1024 devices in a mesh: gx: 16 (over z, core), gy: 64 (over y, x).
Axes of the slice: x: 8, y: 8, z: 8, core: 2. Of those that a mesh axis runs over, the one named last changes fastest.
Arguments:
- start_field: float32 [64, 32, 256, 128], P(None, 'gx', 'gy'), may hold values from -6 to 6
- right_side: float32 [64, 32, 256, 128], P(None, 'gx', 'gy'), may hold values from -6 to 6
- coefficient: float32 [32, 256, 128], P('gx', 'gy'), may hold values from 1 to 10
- stiffness: float32 [64, 64], replicated, may hold values from -0.6 to 4.6, as said below
- smoother: float32 [64, 64], replicated, may hold values from -0.03 to 0.23, as said below
- face_coupling: float32 [6, 64, 64], replicated, may hold values from -0.12 to 0.12
- prolongation: float32 [2, 2, 2, 64, 64], replicated, may hold values from -0.75 to 0.75
Outputs:
- solution_field: float32 [64, 32, 256, 128], P(None, 'gx', 'gy')
The draws below stay inside these ranges and needn't reach their ends.
Inputs may be any that keep to these rules, and one draw needn't show every extreme that they name: `stiffness`: diagonal entries lie in 3.4 to 4.6, the others in -0.6 to 0.6. `smoother`: diagonal entries lie in 0.17 to 0.23, the others in -0.03 to 0.03.
All inputs are finite; a program needn't handle non-finite values.
Results may differ from the reference program's by a relative error of at most 0.00015.
Values sent between devices are 32-bit elements; how exact they have to be, the bound alone decides.
A program may use at most 32 MiB of HBM per device.

```python
import math
import jax
import jax.numpy as jnp
from jax import lax

DOFS = 64
NU = 2
CS = 2
NX = 32
NY = 256
NZ = 128


def coupling_part(key):
    values = jax.random.normal(key, (DOFS, DOFS), jnp.float32)
    return jnp.clip(values, -4.0, 4.0) * 0.15


def draw_stiffness(key, part):
    shared = coupling_part(key)
    identity = jnp.eye(DOFS, dtype=jnp.float32)
    return 4.0 * identity + shared


def draw_smoother(key, part):
    shared = coupling_part(key)
    identity = jnp.eye(DOFS, dtype=jnp.float32)
    return 0.8 * (0.25 * identity - shared / 16.0)


def block_levels(rng, shape, pieces, low, top_value):
    gain, own = 1.0, jax.random.fold_in(rng, 6)
    for dim, blocks in pieces:
        draws = jnp.exp(jax.random.uniform(jax.random.fold_in(own, dim), (blocks,), jnp.float32, low / len(pieces), top_value / len(pieces)))
        gain = gain * jnp.repeat(draws, shape[dim] // blocks).reshape([-1 if axis == dim else 1 for axis in range(len(shape))])
    return gain


def bell_draw(stream_key, shape, scale, most, pieces=(), kind=jnp.bfloat16):
    drawn = jax.random.normal(stream_key, shape, jnp.float32) * scale
    if len(pieces) > 0:
        drawn = block_levels(stream_key, shape, pieces, -0.22, 0.18) * drawn
    return jnp.clip(drawn, min=-most, max=most).astype(kind)


def setup_inputs(seed: int = 0) -> dict:
    splits = jax.random.split(jax.random.key(seed), 8)
    start_field = bell_draw(splits[0], (DOFS, NX, NY, NZ), 1.0, 6.0, ((1, 16), (2, 64)), jnp.float32)
    right_side = bell_draw(splits[1], (DOFS, NX, NY, NZ), 1.0, 6.0, ((1, 16), (2, 64)), jnp.float32)
    coefficient = jnp.clip(jnp.exp(math.log(10.0) - 2.3025851 * jax.random.uniform(splits[2], (NX, NY, NZ), jnp.float32) ** block_levels(splits[2], (NX, NY, NZ), ((0, 16), (1, 64)), -0.2, 0.2)), 1.0, 10.0)
    stiffness = draw_stiffness(jax.random.fold_in(splits[7], 71), 0)
    smoother = draw_smoother(jax.random.fold_in(splits[7], 71), 0)
    face_coupling = bell_draw(splits[5], (6, DOFS, DOFS), 0.02, 0.12, (), jnp.float32)
    prolongation = bell_draw(splits[6], (2, 2, 2, DOFS, DOFS), DOFS ** -0.5, 0.75, (), jnp.float32)
    return dict(start_field=start_field, right_side=right_side, coefficient=coefficient, stiffness=stiffness, smoother=smoother, face_coupling=face_coupling, prolongation=prolongation)


HIGH = lax.Precision.HIGHEST


def block_apply(matrix, field):
    return jnp.einsum('ij,jxyz->ixyz', matrix, field, precision=HIGH)


def stencil(padded, kpad, stiffness, face_coupling):
    sx = padded.shape[1]
    sy = padded.shape[2]
    sz = padded.shape[3]
    sizes = (sx, sy, sz)
    center = padded[:, 1:-1, 1:-1, 1:-1]
    kcenter = kpad[1:-1, 1:-1, 1:-1]
    result = kcenter * block_apply(stiffness, center)
    for axis in range(3):
        for side in range(2):
            offset = 2 * side - 1
            index = [slice(1, sizes[0] - 1), slice(1, sizes[1] - 1), slice(1, sizes[2] - 1)]
            index[axis] = slice(1 + offset, sizes[axis] - 1 + offset)
            nfield = padded[:, index[0], index[1], index[2]]
            ncoef = kpad[index[0], index[1], index[2]]
            weight = 2.0 * kcenter * ncoef / (kcenter + ncoef)
            result = result - weight * block_apply(face_coupling[2 * axis + side], nfield)
    return result


def operate(field, coef, stiffness, face_coupling):
    padded = jnp.pad(field, ((0, 0), (1, 1), (1, 1), (1, 1)))
    kpad = jnp.pad(coef, 1)
    return stencil(padded, kpad, stiffness, face_coupling)


def sweep(field, rhs, coef, stiffness, smoother, face_coupling):
    resid = rhs - operate(field, coef, stiffness, face_coupling)
    return field + block_apply(smoother, resid) / coef


def restrict(resid, coef, prolongation):
    dofs, sx, sy, sz = resid.shape
    parts = resid.reshape(dofs, sx // 2, 2, sy // 2, 2, sz // 2, 2)
    coarse_rhs = jnp.einsum('abcij,ixaybzc->jxyz', prolongation, parts, precision=HIGH)
    coarse_coef = coef.reshape(sx // 2, 2, sy // 2, 2, sz // 2, 2).mean(axis=(1, 3, 5))
    return coarse_rhs, coarse_coef


def lift(correction, prolongation):
    dofs, sx, sy, sz = correction.shape
    fine = jnp.einsum('abcij,jxyz->ixaybzc', prolongation, correction, precision=HIGH)
    return fine.reshape(dofs, 2 * sx, 2 * sy, 2 * sz)


def reference(start_field, right_side, coefficient, stiffness, smoother, face_coupling, prolongation):
    field = start_field
    for step in range(NU):
        field = sweep(field, right_side, coefficient, stiffness, smoother, face_coupling)
    resid = right_side - operate(field, coefficient, stiffness, face_coupling)
    coarse_rhs, coarse_coef = restrict(resid, coefficient, prolongation)
    correction = jnp.zeros_like(coarse_rhs)
    for step in range(CS):
        correction = sweep(correction, coarse_rhs, coarse_coef, stiffness, smoother, face_coupling)
    field = field + lift(correction, prolongation)
    for step in range(NU):
        field = sweep(field, right_side, coefficient, stiffness, smoother, face_coupling)
    return field
```

```python
import jax
import jax.numpy as jnp
from jax import lax
from jax.experimental import pallas as pl
from jax.experimental.pallas import tpu as pltpu
from jax.sharding import PartitionSpec as P

MESH = pl.DeviceIdType.MESH
F32 = jnp.float32
BF16 = jnp.bfloat16
D = 64
L = 128
XLO, CEN, ZLO, ZHI, YLO, YHI, XHI = range(7)


def parts(x):
    hi = x.astype(BF16)
    lo = (x - hi.astype(F32)).astype(BF16)
    return hi, lo


def split_rows(x):
    hi, lo = parts(x)
    return jnp.concatenate([hi, hi, lo, lo], axis=0)


def dot(a, b):
    return jnp.dot(a, b, preferred_element_type=F32)


def roll(x, shift, axis=1):
    return pltpu.roll(x, shift % x.shape[axis], axis)


def col(c):
    return slice(c * L, (c + 1) * L)


def kernel(nx, ny, v_in, b_in, k_in, s_in, m_in, f_in, p_in, out,
           v_raw, b_raw, k_raw, s_raw, m_raw, f_raw, p_raw,
           v0, v1, v2, v3, rhs, const, res, lifted, part, prod,
           hx, hy, hk, c1, c2, hc1, hc2,
           gst, rst, pst, qst, alpha, calpha, krow, local_sem, send_sem, recv_sem):
    gx, gy = lax.axis_index("gx"), lax.axis_index("gy")
    right = (lax.rem(gx + 1, nx), gy)
    left = (lax.rem(gx + nx - 1, nx), gy)
    up = (gx, lax.rem(gy + 1, ny))
    down = (gx, lax.rem(gy + ny - 1, ny))

    loads = [pltpu.make_async_copy(src, dst, local_sem.at[i]) for i, (src, dst) in enumerate(
        ((v_in, v_raw), (k_in, k_raw), (m_in, m_raw), (s_in, s_raw), (f_in, f_raw), (b_in, b_raw), (p_in, p_raw)))]
    for load in loads:
        load.start()
    barrier = pltpu.get_barrier_semaphore()
    for other in (left, right, down, up):
        pl.semaphore_signal(barrier, inc=1, device_id=other, device_id_type=MESH)

    sent = []

    def send(src, dst, device):
        slot = len(sent)
        copy = pltpu.make_async_remote_copy(
            src_ref=src, dst_ref=dst, send_sem=send_sem.at[slot], recv_sem=recv_sem.at[slot],
            device_id=device, device_id_type=MESH)
        copy.start()
        sent.append(copy)
        return copy

    def exchange(v, step):
        lo = [send(v.at[:, 4 * L:], hx.at[step, 0], right)]
        hi = [send(v.at[:, :4 * L], hx.at[step, 1], left)]
        ylo = [send(v.at[:, col(4 * x + 3)], hy.at[step, 0, :, col(x)], up) for x in range(2)]
        yhi = [send(v.at[:, col(4 * x)], hy.at[step, 1, :, col(x)], down) for x in range(2)]
        return lo, hi, ylo, yhi

    def exchange_coarse(c, h):
        return (send(c, h.at[0], right), send(c, h.at[1], left), send(c, h.at[2], up), send(c, h.at[3], down))

    def arrive(copies):
        for copy in copies:
            copy.wait_recv()

    loads[0].wait()
    for c in range(8):
        v0[:, col(c)] = v_raw[pl.ds(c, D, stride=8), :]
    loads[1].wait()
    pl.semaphore_wait(barrier, 4)
    kcopies = [send(k_raw, hk.at[0], right), send(k_raw, hk.at[1], left),
               send(k_raw, hk.at[2], up), send(k_raw, hk.at[3], down)]
    first = exchange(v0, 0)

    lane = lax.broadcasted_iota(jnp.int32, (D, L), 1)
    low_half = lane < D
    even = lax.rem(lane, 2) == 0
    row_even = even[:1]

    def twice(w):
        return jnp.concatenate([w, w], axis=1)

    def put_left(ref, rows, w, lanes=0):
        hi, lo = parts(w)
        both = jnp.where(low_half, hi.astype(F32), lo.astype(F32)).astype(BF16)
        ref[rows, lanes:lanes + L] = both
        ref[rows, lanes + L:lanes + 2 * L] = both

    def block(i):
        return slice(i * D, (i + 1) * D)

    for i in (2, 3, 4):
        loads[i].wait()
    m_hi, m_lo = parts(twice(m_raw[...]))
    m_both = jnp.where(low_half, m_hi.astype(F32), m_lo.astype(F32)).astype(BF16)
    m_left = jnp.concatenate([m_both, m_both], axis=1)
    order = ((XLO, 0), (XHI, 1), (YLO, 2), (YHI, 3), (ZLO, 4), (ZHI, 5))
    raw = {CEN: twice(s_raw[...])}
    for blk, face in order:
        raw[blk] = twice(f_raw[face])
    stacked = jnp.concatenate([raw[blk] for blk in range(7)], axis=1)
    folded = dot(m_left, split_rows(stacked))
    eye = (lax.rem(lane, D) == lax.broadcasted_iota(jnp.int32, (D, L), 0)).astype(F32)
    for blk in range(7):
        w = folded[:, col(blk)]
        put_left(gst, block(blk), eye - w if blk == CEN else w)

    loads[5].wait()
    k8 = k_raw[...]
    inv8 = 1.0 / k8

    def to_row(x8):
        return jnp.concatenate([x8[c:c + 1] for c in range(8)], axis=1)

    krow[0:1, :] = to_row(k8)
    inv_row = to_row(inv8)
    for c in range(8):
        rhs[:, col(c)] = b_raw[pl.ds(c, D, stride=8), :]
    const[...] = dot(m_left, split_rows(rhs[...])) * inv_row

    arrive(kcopies)
    row8 = lax.broadcasted_iota(jnp.int32, (8, L), 0)
    lane8 = lax.broadcasted_iota(jnp.int32, (8, L), 1)
    y8 = lax.rem(row8, 4)
    inside_xlo = (gx > 0).astype(F32)
    inside_xhi = (gx < nx - 1).astype(F32)
    inside_ylo = (gy > 0).astype(F32)
    inside_yhi = (gy < ny - 1).astype(F32)
    kxlo, kxhi = hk[0] * inside_xlo, hk[1] * inside_xhi
    kylo, kyhi = hk[2] * inside_ylo, hk[3] * inside_yhi
    neighbours = {
        XLO: jnp.where(row8 < 4, roll(kxlo, 4, 0), roll(k8, 4, 0)),
        XHI: jnp.where(row8 < 4, roll(k8, 4, 0), roll(kxhi, 4, 0)),
        YLO: jnp.where(y8 == 0, roll(kylo, -3, 0), roll(k8, 1, 0)),
        YHI: jnp.where(y8 == 3, roll(kyhi, 3, 0), roll(k8, -1, 0)),
        ZLO: jnp.where(lane8 == 0, 0.0, roll(k8, 1)),
        ZHI: jnp.where(lane8 == L - 1, 0.0, roll(k8, -1)),
    }
    for blk, kn in neighbours.items():
        alpha[blk:blk + 1, :] = to_row(2.0 * kn / (k8 + kn))

    def weight(blk, c):
        return alpha[blk:blk + 1, col(c)]

    def own_part(v, stack, base, scale):
        x = split_rows(v[...])
        prod[:, :4 * L] = dot(stack[0:6 * D, :], x[:, :4 * L])
        prod[:, 4 * L:] = dot(stack[D:7 * D, :], x[:, 4 * L:])
        for c in range(8):
            plane, y = divmod(c, 4)

            def term(blk, at):
                return prod[block(blk - at // 4), col(at)]

            acc = term(CEN, c)
            acc += weight(ZLO, c) * roll(term(ZLO, c), 1)
            acc += weight(ZHI, c) * roll(term(ZHI, c), -1)
            if plane == 0:
                acc += weight(XHI, c) * term(XHI, c + 4)
            else:
                acc += weight(XLO, c) * term(XLO, c - 4)
            if y > 0:
                acc += weight(YLO, c) * term(YLO, c - 1)
            if y < 3:
                acc += weight(YHI, c) * term(YHI, c + 1)
            if scale is not None:
                acc = acc * scale[0:1, col(c)]
            part[:, col(c)] = base[:, col(c)] + acc

    def halo_part(target, stack, copies, xlo, xhi, ylo, yhi, scale):
        arrive(copies[2])
        from_ylo = dot(stack[block(YLO), :], split_rows(ylo[...]))
        arrive(copies[3])
        from_yhi = dot(stack[block(YHI), :], split_rows(yhi[...]))
        arrive(copies[0])
        from_xlo = dot(stack[block(XLO), :], split_rows(xlo[...]))
        arrive(copies[1])
        from_xhi = dot(stack[block(XHI), :], split_rows(xhi[...]))
        for c in range(8):
            plane, y = divmod(c, 4)
            if plane == 0:
                acc = weight(XLO, c) * from_xlo[:, col(y)]
            else:
                acc = weight(XHI, c) * from_xhi[:, col(y)]
            if y == 0:
                acc += weight(YLO, c) * from_ylo[:, col(plane)]
            if y == 3:
                acc += weight(YHI, c) * from_yhi[:, col(plane)]
            if scale is not None:
                acc = acc * scale[0:1, col(c)]
            value = part[:, col(c)] + acc
            if target is out:
                out[pl.ds(c, D, stride=8), :] = value
            else:
                target[:, col(c)] = value

    nothing = ((), (), (), ())

    own_part(v0, gst, const, None)
    halo_part(v1, gst, first, hx.at[0, 0], hx.at[0, 1], hy.at[0, 0], hy.at[0, 1], None)
    second = exchange(v1, 1)
    own_part(v1, gst, const, None)

    for blk in range(7):
        put_left(rst, block(blk), -raw[blk] if blk == CEN else raw[blk])
    loads[6].wait()
    twins = []
    for abc in range(8):
        w = twice(p_raw[abc])
        put_left(pst, block(abc), w)
        hi, lo = parts(w)
        right_form = jnp.concatenate([hi, lo], axis=1)
        twins += [right_form, right_form]
    folded_p = lax.dot_general(m_left, jnp.concatenate(twins, axis=0), (((1,), (1,)), ((), ())),
                               preferred_element_type=F32)
    for abc in range(8):
        ab, c = divmod(abc, 2)
        put_left(qst, block(c), folded_p[:, col(abc)], 2 * L * ab)

    def coarse_k(k):
        def one(q):
            s = (k[2 * q:2 * q + 1] + k[2 * q + 1:2 * q + 2]) + (k[4 + 2 * q:5 + 2 * q] + k[5 + 2 * q:6 + 2 * q])
            return (s + roll(s, -1)) * 0.125

        return jnp.where(row_even, one(0), roll(one(1), 1))

    kc = coarse_k(k8)
    lane1 = lax.broadcasted_iota(jnp.int32, (1, L), 1)
    cylo, cyhi = coarse_k(kylo), coarse_k(kyhi)
    coarse_neighbours = {
        XLO: coarse_k(kxlo),
        XHI: coarse_k(kxhi),
        YLO: jnp.where(row_even, roll(cylo, -1), roll(kc, 1)),
        YHI: jnp.where(row_even, roll(kc, -1), roll(cyhi, 1)),
        ZLO: jnp.where(lane1 < 2, 0.0, roll(kc, 2)),
        ZHI: jnp.where(lane1 >= L - 2, 0.0, roll(kc, -2)),
    }
    for blk, kn in coarse_neighbours.items():
        calpha[blk:blk + 1, :] = 2.0 * kn / (kc + kn)
    inv_kc = 1.0 / kc

    halo_part(v2, gst, second, hx.at[1, 0], hx.at[1, 1], hy.at[1, 0], hy.at[1, 1], None)

    third = exchange(v2, 2)
    own_part(v2, rst, rhs, krow)
    halo_part(res, rst, third, hx.at[2, 0], hx.at[2, 1], hy.at[2, 0], hy.at[2, 1], krow)
    r_right = split_rows(res[...])
    columns = []
    for a in range(2):
        for b in range(2):
            columns.append(jnp.concatenate([r_right[:, col(4 * a + b)], r_right[:, col(4 * a + 2 + b)]], axis=1))
    t = dot(qst[...], jnp.concatenate(columns, axis=0))
    packed = jnp.where(even, t[:D, :L] + roll(t[D:, :L], -1), roll(t[:D, L:], 1) + t[D:, L:])
    c1[...] = packed * inv_kc

    fourth = exchange_coarse(c1, hc1)
    corr1 = c1[...]
    y = dot(gst[D:4 * D, :], split_rows(corr1))
    acc = corr1 + y[:D]
    acc += calpha[ZLO:ZLO + 1, :] * roll(y[D:2 * D], 2)
    acc += calpha[ZHI:ZHI + 1, :] * roll(y[2 * D:], -2)
    arrive(fourth[2:3])
    below = jnp.where(even, roll(hc1[2], -1), roll(corr1, 1))
    acc += calpha[YLO:YLO + 1, :] * dot(gst[block(YLO), :], split_rows(below))
    arrive(fourth[3:4])
    above = jnp.where(even, roll(corr1, -1), roll(hc1[3], 1))
    acc += calpha[YHI:YHI + 1, :] * dot(gst[block(YHI), :], split_rows(above))
    arrive(fourth[0:1])
    acc += calpha[XLO:XLO + 1, :] * dot(gst[block(XLO), :], split_rows(hc1[0]))
    arrive(fourth[1:2])
    acc += calpha[XHI:XHI + 1, :] * dot(gst[block(XHI), :], split_rows(hc1[1]))
    c2[...] = acc

    fifth = exchange_coarse(c2, hc2)

    def lift(o, q):
        if q == 0:
            return jnp.where(even, o[:D], roll(o[D:], 1))
        return jnp.where(even, roll(o[:D], -1), o[D:])

    def pair(o, i):
        return o[2 * i * D:2 * (i + 1) * D]

    o = dot(pst[...], split_rows(c2[...]))
    for c in range(8):
        plane, y = divmod(c, 4)
        q, b = divmod(y, 2)
        lifted[:, col(c)] = v2[:, col(c)] + lift(pair(o, 2 * plane + b), q)
    own_part(lifted, gst, const, None)
    arrive(fifth[2:3])
    o = dot(pst[...], split_rows(hc2[2]))
    for a in range(2):
        hy[2, 0, :, col(a)] = hy[2, 0, :, col(a)] + lift(pair(o, 2 * a + 1), 1)
    arrive(fifth[3:4])
    o = dot(pst[...], split_rows(hc2[3]))
    for a in range(2):
        hy[2, 1, :, col(a)] = hy[2, 1, :, col(a)] + lift(pair(o, 2 * a), 0)
    arrive(fifth[0:1])
    o = dot(pst[4 * D:, :], split_rows(hc2[0]))
    for y in range(4):
        hx[2, 0, :, col(y)] = hx[2, 0, :, col(y)] + lift(pair(o, y % 2), y // 2)
    arrive(fifth[1:2])
    o = dot(pst[:4 * D, :], split_rows(hc2[1]))
    for y in range(4):
        hx[2, 1, :, col(y)] = hx[2, 1, :, col(y)] + lift(pair(o, y % 2), y // 2)
    halo_part(v3, gst, nothing, hx.at[2, 0], hx.at[2, 1], hy.at[2, 0], hy.at[2, 1], None)
    last = exchange(v3, 3)
    own_part(v3, gst, const, None)
    halo_part(out, gst, last, hx.at[3, 0], hx.at[3, 1], hy.at[3, 0], hy.at[3, 1], None)
    for copy in sent:
        copy.wait_send()


def on_device(nx, ny, start_field, right_side, coefficient, stiffness, smoother, face_coupling, prolongation):
    flat = lambda x: x.reshape(8 * D, L)
    field = pltpu.VMEM((D, 8 * L), F32)
    small = pltpu.VMEM((D, L), F32)
    sends = 4 + 4 * 6 + 2 * 4

    def body(*refs):
        kernel(nx, ny, *refs)

    result = pl.pallas_call(
        body,
        out_shape=jax.ShapeDtypeStruct((8 * D, L), F32),
        in_specs=[pl.BlockSpec(memory_space=pl.ANY)] * 7,
        out_specs=pl.BlockSpec(memory_space=pltpu.VMEM),
        scratch_shapes=[
            pltpu.VMEM((8 * D, L), F32), pltpu.VMEM((8 * D, L), F32), pltpu.VMEM((8, L), F32),
            pltpu.VMEM((D, D), F32), pltpu.VMEM((D, D), F32), pltpu.VMEM((6, D, D), F32), pltpu.VMEM((8, D, D), F32),
            field, field, field, field, field, field, field, field, field, pltpu.VMEM((6 * D, 8 * L), F32),
            pltpu.VMEM((4, 2, D, 4 * L), F32), pltpu.VMEM((4, 2, D, 2 * L), F32), pltpu.VMEM((4, 8, L), F32),
            small, small, pltpu.VMEM((4, D, L), F32), pltpu.VMEM((4, D, L), F32),
            pltpu.VMEM((7 * D, 4 * D), BF16), pltpu.VMEM((7 * D, 4 * D), BF16),
            pltpu.VMEM((8 * D, 4 * D), BF16), pltpu.VMEM((2 * D, 16 * D), BF16),
            pltpu.VMEM((8, 8 * L), F32), pltpu.VMEM((8, L), F32), pltpu.VMEM((8, 8 * L), F32),
            pltpu.SemaphoreType.DMA((7,)), pltpu.SemaphoreType.DMA((sends,)), pltpu.SemaphoreType.DMA((sends,)),
        ],
        compiler_params=pltpu.CompilerParams(
            collective_id=0, has_side_effects=True, vmem_limit_bytes=40 * 2**20),
    )(flat(start_field), flat(right_side), coefficient.reshape(8, L), stiffness, smoother, face_coupling,
      prolongation.reshape(8, D, D))
    return result.reshape(start_field.shape)


def solution(mesh):
    nx, ny = mesh.shape["gx"], mesh.shape["gy"]
    placed = (P(None, "gx", "gy", None), P(None, "gx", "gy", None), P("gx", "gy", None), P(), P(), P(), P())

    def run(*args):
        return on_device(nx, ny, *args)

    return jax.shard_map(
        run, mesh=mesh, in_specs=placed, out_specs=P(None, "gx", "gy", None), check_vma=False)
```

```python
import jax
import jax.numpy as jnp
from jax import lax
from jax.experimental import pallas as pl
from jax.experimental.pallas import tpu as pltpu
from jax.sharding import PartitionSpec as P

MESH = pl.DeviceIdType.MESH
F32 = jnp.float32
BF16 = jnp.bfloat16
D = 64
L = 128
XLO, CEN, ZLO, ZHI, YLO, YHI, XHI = range(7)


def parts(x):
    hi = x.astype(BF16)
    lo = (x - hi.astype(F32)).astype(BF16)
    return hi, lo


def split_rows(x):
    hi, lo = parts(x)
    return jnp.concatenate([hi, hi, lo, lo], axis=0)


def dot(a, b):
    return jnp.dot(a, b, preferred_element_type=F32)


def roll(x, shift, axis=1):
    return pltpu.roll(x, shift % x.shape[axis], axis)


def col(c):
    return slice(c * L, (c + 1) * L)


def kernel(nx, ny, v_in, b_in, k_in, s_in, m_in, f_in, p_in, out,
           v_raw, b_raw, k_raw, s_raw, m_raw, f_raw, p_raw,
           v0, v1, v2, v3, rhs, const, res, lifted, part0, part1, part2, part3, prod,
           hx0, hy0, hx1, hy1, hpx1, hpy1, hx2, hy2, hpx3, hpy3, hx3, hy3, edge1, edge3, hk, hkc, c1, c2, hc1, hc2,
           gst, rst, pst, qst, alpha, calpha, krow, local_sem, send_sem, recv_sem):
    gx, gy = lax.axis_index("gx"), lax.axis_index("gy")
    has = {(-1, 0): gx > 0, (1, 0): gx < nx - 1, (0, -1): gy > 0, (0, 1): gy < ny - 1}
    for dx in (-1, 1):
        for dy in (-1, 1):
            has[dx, dy] = jnp.logical_and(has[dx, 0], has[0, dy])
    faces = ((0, -1), (0, 1), (-1, 0), (1, 0))
    diagonals = ((-1, -1), (-1, 1), (1, -1), (1, 1))

    loads = [pltpu.make_async_copy(src, dst, local_sem.at[i]) for i, (src, dst) in enumerate(
        ((v_in, v_raw), (k_in, k_raw), (m_in, m_raw), (s_in, s_raw), (f_in, f_raw), (b_in, b_raw), (p_in, p_raw)))]
    barrier = pltpu.get_barrier_semaphore()
    for d in faces:
        @pl.when(has[d])
        def _(d=d):
            pl.semaphore_signal(barrier, inc=1, device_id=(gx + d[0], gy + d[1]), device_id_type=MESH)
    for load in loads:
        load.start()

    sent = []

    def send(src, dst, d):
        slot = len(sent)
        copy = pltpu.make_async_remote_copy(
            src_ref=src, dst_ref=dst, send_sem=send_sem.at[slot], recv_sem=recv_sem.at[slot],
            device_id=(gx + d[0], gy + d[1]), device_id_type=MESH)
        pl.when(has[d])(copy.start)
        sent.append((copy, d))
        return copy, (-d[0], -d[1])

    def arrive(*copies):
        for copy, source in copies:
            pl.when(has[source])(copy.wait_recv)

    def send_columns(v, hx, hy):
        return (send(v.at[:, :, col(3)], hy.at[0], (0, 1)), send(v.at[:, :, col(0)], hy.at[1], (0, -1)),
                send(v.at[1], hx.at[0], (1, 0)), send(v.at[0], hx.at[1], (-1, 0)))

    def send_edges(v, edge):
        return [send(v.at[(1 + dx) // 2, :, col(3 if dy > 0 else 0)], edge.at[(1 - dx) + (1 - dy) // 2], (dx, dy))
                for dx, dy in diagonals]

    def send_tile(c, h):
        return (send(c, h.at[0], (0, 1)), send(c, h.at[1], (0, -1)), send(c, h.at[2], (1, 0)), send(c, h.at[3], (-1, 0)))

    for d, y_at, x_at in (((0, -1), 0, None), ((0, 1), 1, None), ((-1, 0), None, 0), ((1, 0), None, 1)):
        @pl.when(jnp.logical_not(has[d]))
        def _(y_at=y_at, x_at=x_at):
            if x_at is None:
                for ref in (hy0, hy1, hpy1, hpy3):
                    ref[y_at] = jnp.zeros_like(ref[y_at])
                for ref in (hk, hc1, hc2):
                    ref[y_at] = jnp.zeros_like(ref[y_at])
                for i in range(2):
                    for ref in (edge1, edge3, hkc):
                        ref[2 * i + y_at] = jnp.zeros_like(ref[0])
            else:
                for ref in (hx0, hx1, hpx1, hpx3):
                    ref[x_at] = jnp.zeros_like(ref[x_at])
                for ref in (hk, hc1, hc2):
                    ref[2 + x_at] = jnp.zeros_like(ref[0])
                for j in range(2):
                    for ref in (edge1, edge3, hkc):
                        ref[2 * x_at + j] = jnp.zeros_like(ref[0])

    loads[0].wait()
    for c in range(8):
        v0[c // 4, :, col(c % 4)] = v_raw[pl.ds(c, D, stride=8), :]
    loads[1].wait()
    count = has[-1, 0].astype(jnp.int32) + has[1, 0].astype(jnp.int32) + has[0, -1].astype(jnp.int32) + has[0, 1].astype(jnp.int32)
    pl.semaphore_wait(barrier, count)
    first = send_columns(v0, hx0, hy0)
    kcopies = send_tile(k_raw, hk)

    lane = lax.broadcasted_iota(jnp.int32, (D, L), 1)
    low_half = lane < D
    even = lax.rem(lane, 2) == 0
    row_even = even[:1]

    def twice(w):
        return jnp.concatenate([w, w], axis=1)

    def put_left(ref, rows, w, lanes=0):
        hi, lo = parts(w)
        both = jnp.where(low_half, hi.astype(F32), lo.astype(F32)).astype(BF16)
        ref[rows, lanes:lanes + L] = both
        ref[rows, lanes + L:lanes + 2 * L] = both

    def block(i):
        return slice(i * D, (i + 1) * D)

    for i in (2, 3, 4):
        loads[i].wait()
    m_hi, m_lo = parts(twice(m_raw[...]))
    m_both = jnp.where(low_half, m_hi.astype(F32), m_lo.astype(F32)).astype(BF16)
    m_left = jnp.concatenate([m_both, m_both], axis=1)
    order = ((XLO, 0), (XHI, 1), (YLO, 2), (YHI, 3), (ZLO, 4), (ZHI, 5))
    raw = {CEN: twice(s_raw[...])}
    for blk, face in order:
        raw[blk] = twice(f_raw[face])
    stacked = jnp.concatenate([raw[blk] for blk in range(7)], axis=1)
    folded = dot(m_left, split_rows(stacked))
    eye = (lax.rem(lane, D) == lax.broadcasted_iota(jnp.int32, (D, L), 0)).astype(F32)
    for blk in range(7):
        w = folded[:, col(blk)]
        put_left(gst, block(blk), eye - w if blk == CEN else w)

    loads[5].wait()
    k8 = k_raw[...]
    inv8 = 1.0 / k8
    for c in range(8):
        krow[c // 4, 0:1, col(c % 4)] = k8[c:c + 1]
        krow[c // 4, 1:2, col(c % 4)] = inv8[c:c + 1]
        rhs[c // 4, :, col(c % 4)] = b_raw[pl.ds(c, D, stride=8), :]
    for x in range(2):
        const[x] = dot(m_left, split_rows(rhs[x])) * krow[x, 1:2, :]

    def weigh(ke, kn):
        return jnp.where(kn > 0, 2.0 * kn / (ke + kn), 0.0)

    def weight(blk, c):
        return alpha[blk, c:c + 1, :]

    for blk in range(7):
        put_left(rst, block(blk), -raw[blk] if blk == CEN else raw[blk])
    loads[6].wait()
    twins = []
    for abc in range(8):
        w = twice(p_raw[abc])
        put_left(pst, block(abc), w)
        hi, lo = parts(w)
        right_form = jnp.concatenate([hi, lo], axis=1)
        twins += [right_form, right_form]
    folded_p = lax.dot_general(m_left, jnp.concatenate(twins, axis=0), (((1,), (1,)), ((), ())),
                               preferred_element_type=F32)
    for abc in range(8):
        ab, c = divmod(abc, 2)
        put_left(qst, block(c), folded_p[:, col(abc)], 2 * L * ab)

    arrive(*kcopies)
    row8 = lax.broadcasted_iota(jnp.int32, (8, L), 0)
    lane8 = lax.broadcasted_iota(jnp.int32, (8, L), 1)
    y8 = lax.rem(row8, 4)
    kylo, kyhi, kxlo, kxhi = (hk[i] for i in range(4))
    neighbours = {
        XLO: jnp.where(row8 < 4, roll(kxlo, 4, 0), roll(k8, 4, 0)),
        XHI: jnp.where(row8 < 4, roll(k8, 4, 0), roll(kxhi, 4, 0)),
        YLO: jnp.where(y8 == 0, roll(kylo, -3, 0), roll(k8, 1, 0)),
        YHI: jnp.where(y8 == 3, roll(kyhi, 3, 0), roll(k8, -1, 0)),
        ZLO: jnp.where(lane8 == 0, 0.0, roll(k8, 1)),
        ZHI: jnp.where(lane8 == L - 1, 0.0, roll(k8, -1)),
    }
    for blk, kn in neighbours.items():
        alpha[blk] = weigh(k8, kn)

    def coarse_k(k):
        def one(q):
            s = (k[2 * q:2 * q + 1] + k[2 * q + 1:2 * q + 2]) + (k[4 + 2 * q:5 + 2 * q] + k[5 + 2 * q:6 + 2 * q])
            return (s + roll(s, -1)) * 0.125

        return jnp.where(row_even, one(0), roll(one(1), 1))

    kc = coarse_k(k8)
    lane1 = lax.broadcasted_iota(jnp.int32, (1, L), 1)
    cylo, cyhi = coarse_k(kylo), coarse_k(kyhi)
    coarse_neighbours = {
        XLO: coarse_k(kxlo),
        XHI: coarse_k(kxhi),
        YLO: jnp.where(row_even, roll(cylo, -1), roll(kc, 1)),
        YHI: jnp.where(row_even, roll(kc, -1), roll(cyhi, 1)),
        ZLO: jnp.where(lane1 < 2, 0.0, roll(kc, 2)),
        ZHI: jnp.where(lane1 >= L - 2, 0.0, roll(kc, -2)),
    }
    for blk, kn in coarse_neighbours.items():
        calpha[blk:blk + 1, :] = weigh(kc, kn)
    inv_kc = 1.0 / kc

    def own_part(target, v, stack, base, scale, wide):
        for x in range(2):
            rows = slice(0, 7 * D) if wide else slice(x * D, (6 + x) * D)
            prod[x, rows, :] = dot(stack[rows, :], split_rows(v[x]))
        for c in range(8):
            x, y = divmod(c, 4)

            def term(blk, x, y):
                return prod[x, block(blk), col(y)]

            acc = term(CEN, x, y)
            acc += weight(ZLO, c) * roll(term(ZLO, x, y), 1)
            acc += weight(ZHI, c) * roll(term(ZHI, x, y), -1)
            if x == 0:
                acc += weight(XHI, c) * term(XHI, 1, y)
            else:
                acc += weight(XLO, c) * term(XLO, 0, y)
            if y > 0:
                acc += weight(YLO, c) * term(YLO, x, y - 1)
            if y < 3:
                acc += weight(YHI, c) * term(YHI, x, y + 1)
            if scale is not None:
                acc = acc * scale[x, 0:1, col(y)]
            target[x, :, col(y)] = base[x, :, col(y)] + acc

    def halo_part(target, part, stack, hx, hy, copies, scale):
        arrive(*copies[2:3])
        from_xlo = dot(stack[block(XLO), :], split_rows(hx[0]))
        arrive(*copies[3:4])
        from_xhi = dot(stack[block(XHI), :], split_rows(hx[1]))

        def both(h):
            return split_rows(jnp.concatenate([h[0], h[1]], axis=1))

        arrive(*copies[0:1])
        from_ylo = dot(stack[block(YLO), :], both(hy.at[0]))
        arrive(*copies[1:2])
        from_yhi = dot(stack[block(YHI), :], both(hy.at[1]))
        for c in range(8):
            x, y = divmod(c, 4)
            acc = weight(XLO, c) * from_xlo[:, col(y)] if x == 0 else weight(XHI, c) * from_xhi[:, col(y)]
            if y == 0:
                acc += weight(YLO, c) * from_ylo[:, col(x)]
            if y == 3:
                acc += weight(YHI, c) * from_yhi[:, col(x)]
            if scale is not None:
                acc = acc * scale[x, 0:1, col(y)]
            value = part[x, :, col(y)] + acc
            if target is out:
                out[pl.ds(c, D, stride=8), :] = value
            else:
                target[x, :, col(y)] = value

    def complete_halo(hx, hy, hpx, hpy, edge, copies):
        arrive(*copies)

        def edges(i, j):
            return split_rows(jnp.concatenate([edge[i], edge[j]], axis=1))

        from_edge = {XLO: dot(gst[block(XLO), :], edges(0, 1)), XHI: dot(gst[block(XHI), :], edges(2, 3)),
                     YLO: dot(gst[block(YLO), :], edges(0, 2)), YHI: dot(gst[block(YHI), :], edges(1, 3))}
        kx, ky = (kxlo, kxhi), (kylo, kyhi)
        for i in range(2):
            mine, theirs = ((XLO, XHI), (XHI, XLO))[i]
            for y in range(4):
                c = 4 * i + y
                value = hpx[i, :, col(y)] + (2.0 - weight(mine, c)) * prod[i, block(theirs), col(y)]
                if y in (0, 3):
                    j = y // 3
                    w = weigh(kx[i][4 * (1 - i) + y:4 * (1 - i) + y + 1],
                              hkc[2 * i + j][4 * (1 - i) + 3 - y:4 * (1 - i) + 4 - y])
                    value += w * from_edge[(YLO, YHI)[j]][:, col(i)]
                hx[i, :, col(y)] = value
        for j in range(2):
            mine, theirs = ((YLO, YHI), (YHI, YLO))[j]
            y = 3 * j
            for x in range(2):
                value = hpy[j, x] + (2.0 - weight(mine, 4 * x + y)) * prod[x, block(theirs), col(y)]
                e, n = 4 * x + 3 - y, 4 * (1 - x) + 3 - y
                w = weigh(ky[j][e:e + 1], hkc[2 * x + j][n:n + 1])
                value += w * from_edge[(XLO, XHI)[x]][:, col(j)]
                hy[j, x] = value

    own_part(part0, v0, gst, const, None, False)
    halo_part(v1, part0, gst, hx0, hy0, first, None)
    second = send_columns(v1, hx1, hy1)
    edges1 = send_edges(v1, edge1)
    kedges = [send(k_raw, hkc.at[(1 - dx) + (1 - dy) // 2], (dx, dy)) for dx, dy in diagonals]
    own_part(part1, v1, gst, const, None, True)
    parts1 = send_columns(part1, hpx1, hpy1)
    halo_part(v2, part1, gst, hx1, hy1, second, None)
    complete_halo(hx2, hy2, hpx1, hpy1, edge1, [*edges1, *kedges, *parts1])

    own_part(part2, v2, rst, rhs, krow, False)
    halo_part(res, part2, rst, hx2, hy2, ((),) * 0, krow)
    r_right = [split_rows(res[x]) for x in range(2)]
    columns = []
    for a in range(2):
        for b in range(2):
            columns.append(jnp.concatenate([r_right[a][:, col(b)], r_right[a][:, col(2 + b)]], axis=1))
    t = dot(qst[...], jnp.concatenate(columns, axis=0))
    packed = jnp.where(even, t[:D, :L] + roll(t[D:, :L], -1), roll(t[:D, L:], 1) + t[D:, L:])
    c1[...] = packed * inv_kc

    third = send_tile(c1, hc1)
    corr1 = c1[...]
    y = dot(gst[D:4 * D, :], split_rows(corr1))
    acc = corr1 + y[:D]
    acc += calpha[ZLO:ZLO + 1, :] * roll(y[D:2 * D], 2)
    acc += calpha[ZHI:ZHI + 1, :] * roll(y[2 * D:], -2)
    arrive(third[2])
    acc += calpha[XLO:XLO + 1, :] * dot(gst[block(XLO), :], split_rows(hc1[2]))
    arrive(third[3])
    acc += calpha[XHI:XHI + 1, :] * dot(gst[block(XHI), :], split_rows(hc1[3]))
    arrive(third[0])
    below = jnp.where(even, roll(hc1[0], -1), roll(corr1, 1))
    acc += calpha[YLO:YLO + 1, :] * dot(gst[block(YLO), :], split_rows(below))
    arrive(third[1])
    above = jnp.where(even, roll(corr1, -1), roll(hc1[1], 1))
    acc += calpha[YHI:YHI + 1, :] * dot(gst[block(YHI), :], split_rows(above))
    c2[...] = acc

    fourth = send_tile(c2, hc2)

    def lift(o, q):
        if q == 0:
            return jnp.where(even, o[:D], roll(o[D:], 1))
        return jnp.where(even, roll(o[:D], -1), o[D:])

    def pair(o, i):
        return o[2 * i * D:2 * (i + 1) * D]

    o = dot(pst[...], split_rows(c2[...]))
    for c in range(8):
        x, y = divmod(c, 4)
        q, b = divmod(y, 2)
        lifted[x, :, col(y)] = v2[x, :, col(y)] + lift(pair(o, 2 * x + b), q)
    edges3 = send_edges(lifted, edge3)
    own_part(part3, lifted, gst, const, None, True)
    parts3 = send_columns(part3, hpx3, hpy3)
    for i in range(2):
        arrive(fourth[2 + i])
        o = dot(pst[4 * D * (1 - i):4 * D * (2 - i), :], split_rows(hc2[2 + i]))
        for y in range(4):
            hx2[i, :, col(y)] = hx2[i, :, col(y)] + lift(pair(o, y % 2), y // 2)
    for j in range(2):
        arrive(fourth[j])
        o = dot(pst[...], split_rows(hc2[j]))
        for x in range(2):
            hy2[j, x] = hy2[j, x] + lift(pair(o, 2 * x + 1 - j), 1 - j)
    halo_part(v3, part3, gst, hx2, hy2, ((),) * 0, None)
    complete_halo(hx3, hy3, hpx3, hpy3, edge3, [*edges3, *parts3])
    own_part(part0, v3, gst, const, None, False)
    halo_part(out, part0, gst, hx3, hy3, ((),) * 0, None)
    for copy, d in sent:
        pl.when(has[d])(copy.wait_send)


def on_device(nx, ny, start_field, right_side, coefficient, stiffness, smoother, face_coupling, prolongation):
    flat = lambda x: x.reshape(8 * D, L)
    field = pltpu.VMEM((2, D, 4 * L), F32)
    small = pltpu.VMEM((D, L), F32)
    four = pltpu.VMEM((4, D, L), F32)
    kfour = pltpu.VMEM((4, 8, L), F32)
    xhalo = pltpu.VMEM((2, D, 4 * L), F32)
    yhalo = pltpu.VMEM((2, 2, D, L), F32)
    sends = 40

    def body(*refs):
        kernel(nx, ny, *refs)

    result = pl.pallas_call(
        body,
        out_shape=jax.ShapeDtypeStruct((8 * D, L), F32),
        in_specs=[pl.BlockSpec(memory_space=pltpu.HBM)] * 7,
        out_specs=pl.BlockSpec(memory_space=pltpu.VMEM),
        scratch_shapes=[
            pltpu.VMEM((8 * D, L), F32), pltpu.VMEM((8 * D, L), F32), pltpu.VMEM((8, L), F32),
            pltpu.VMEM((D, D), F32), pltpu.VMEM((D, D), F32), pltpu.VMEM((6, D, D), F32), pltpu.VMEM((8, D, D), F32),
            *[field] * 12, pltpu.VMEM((2, 7 * D, 4 * L), F32),
            *[xhalo, yhalo] * 6, four, four, kfour, kfour, small, small, four, four,
            pltpu.VMEM((7 * D, 4 * D), BF16), pltpu.VMEM((7 * D, 4 * D), BF16),
            pltpu.VMEM((8 * D, 4 * D), BF16), pltpu.VMEM((2 * D, 16 * D), BF16),
            pltpu.VMEM((7, 8, L), F32), pltpu.VMEM((8, L), F32), pltpu.VMEM((2, 8, 4 * L), F32),
            pltpu.SemaphoreType.DMA((7,)), pltpu.SemaphoreType.DMA((sends,)), pltpu.SemaphoreType.DMA((sends,)),
        ],
        compiler_params=pltpu.CompilerParams(
            collective_id=0, has_side_effects=True, vmem_limit_bytes=63 * 2**20),
    )(flat(start_field), flat(right_side), coefficient.reshape(8, L), stiffness, smoother, face_coupling,
      prolongation.reshape(8, D, D))
    return result.reshape(start_field.shape)


def solution(mesh):
    nx, ny = mesh.shape["gx"], mesh.shape["gy"]
    placed = (P(None, "gx", "gy", None), P(None, "gx", "gy", None), P("gx", "gy", None), P(), P(), P(), P())

    def run(*args):
        return on_device(nx, ny, *args)

    return jax.shard_map(
        run, mesh=mesh, in_specs=placed, out_specs=P(None, "gx", "gy", None), check_vma=False)
```

```python
import jax
import jax.numpy as jnp
from jax import lax
from jax.experimental import pallas as pl
from jax.experimental.pallas import tpu as pltpu
from jax.sharding import PartitionSpec as P

MESH = pl.DeviceIdType.MESH
F32 = jnp.float32
BF16 = jnp.bfloat16
D = 64
L = 128
XLO, CEN, ZLO, ZHI, YLO, YHI, XHI = range(7)


def parts(x):
    hi = x.astype(BF16)
    lo = (x - hi.astype(F32)).astype(BF16)
    return hi, lo


def split_rows(x):
    hi, lo = parts(x)
    return jnp.concatenate([hi, hi, lo, lo], axis=0)


def dot(a, b):
    return jnp.dot(a, b, preferred_element_type=F32)


def roll(x, shift, axis=1):
    return pltpu.roll(x, shift % x.shape[axis], axis)


def col(c):
    return slice(c * L, (c + 1) * L)


def kernel(nx, ny, v_in, b_in, k_in, s_in, m_in, f_in, p_in, out,
           v_raw, b_raw, k_raw, s_raw, m_raw, f_raw, p_raw,
           v0, v1, v2, v3, rhs, const, res, lifted, part0, part1, part2, part3, prod, prod1,
           hx0, hy0, hx1, hy1, hpx1, hpy1, hx2, hy2, hpx3, hpy3, hx3, hy3, edge1, edge3, hk, hkc, c1, c2, hc1, hc2,
           gst, rst, pst, qst, gpx, gpy, ghx, ghy, alpha, calpha, krow, local_sem, send_sem, recv_sem):
    gx, gy = lax.axis_index("gx"), lax.axis_index("gy")
    has = {(-1, 0): gx > 0, (1, 0): gx < nx - 1, (0, -1): gy > 0, (0, 1): gy < ny - 1}
    for dx in (-1, 1):
        for dy in (-1, 1):
            has[dx, dy] = jnp.logical_and(has[dx, 0], has[0, dy])
    faces = ((0, -1), (0, 1), (-1, 0), (1, 0))
    diagonals = ((-1, -1), (-1, 1), (1, -1), (1, 1))

    loads = [pltpu.make_async_copy(src, dst, local_sem.at[i]) for i, (src, dst) in enumerate(
        ((k_in, k_raw), (v_in, v_raw), (m_in, m_raw), (s_in, s_raw), (f_in, f_raw), (b_in, b_raw), (p_in, p_raw)))]
    barrier = pltpu.get_barrier_semaphore()
    for d in faces:
        @pl.when(has[d])
        def _(d=d):
            pl.semaphore_signal(barrier, inc=1, device_id=(gx + d[0], gy + d[1]), device_id_type=MESH)
    for load in loads:
        load.start()

    sent = []

    def send(src, dst, d):
        slot = len(sent)
        copy = pltpu.make_async_remote_copy(
            src_ref=src, dst_ref=dst, send_sem=send_sem.at[slot], recv_sem=recv_sem.at[slot],
            device_id=(gx + d[0], gy + d[1]), device_id_type=MESH)
        pl.when(has[d])(copy.start)
        sent.append((copy, d))
        return copy, (-d[0], -d[1])

    def arrive(*copies):
        for copy, source in copies:
            pl.when(has[source])(copy.wait_recv)

    def send_y(v, hy):
        return [send(v.at[:, :, col(3)], hy.at[0], (0, 1)), send(v.at[:, :, col(0)], hy.at[1], (0, -1))]

    def send_x(v, hx):
        return [send(v.at[1], hx.at[0], (1, 0)), send(v.at[0], hx.at[1], (-1, 0))]

    def send_edges(v, edge):
        return [send(v.at[(1 + dx) // 2, :, col(3 if dy > 0 else 0)], edge.at[(1 - dx) + (1 - dy) // 2], (dx, dy))
                for dx, dy in diagonals]

    def send_tile(c, h):
        return (send(c, h.at[0], (0, 1)), send(c, h.at[1], (0, -1)), send(c, h.at[2], (1, 0)), send(c, h.at[3], (-1, 0)))

    for d, y_at, x_at in (((0, -1), 0, None), ((0, 1), 1, None), ((-1, 0), None, 0), ((1, 0), None, 1)):
        @pl.when(jnp.logical_not(has[d]))
        def _(y_at=y_at, x_at=x_at):
            if x_at is None:
                for ref in (hy0, hy1, hpy1, hpy3):
                    ref[y_at] = jnp.zeros_like(ref[y_at])
                for ref in (hk, hc1, hc2):
                    ref[y_at] = jnp.zeros_like(ref[y_at])
                for i in range(2):
                    for ref in (edge1, edge3, hkc):
                        ref[2 * i + y_at] = jnp.zeros_like(ref[0])
            else:
                for ref in (hx0, hx1, hpx1, hpx3):
                    ref[x_at] = jnp.zeros_like(ref[x_at])
                for ref in (hk, hc1, hc2):
                    ref[2 + x_at] = jnp.zeros_like(ref[0])
                for j in range(2):
                    for ref in (edge1, edge3, hkc):
                        ref[2 * x_at + j] = jnp.zeros_like(ref[0])

    loads[1].wait()
    for c in range(8):
        v0[c // 4, :, col(c % 4)] = v_raw[pl.ds(c, D, stride=8), :]
    loads[0].wait()
    count = has[-1, 0].astype(jnp.int32) + has[1, 0].astype(jnp.int32) + has[0, -1].astype(jnp.int32) + has[0, 1].astype(jnp.int32)
    pl.semaphore_wait(barrier, count)
    kcopies = send_tile(k_raw, hk)
    first = send_y(v0, hy0) + send_x(v0, hx0)

    lane = lax.broadcasted_iota(jnp.int32, (D, L), 1)
    low_half = lane < D
    even = lax.rem(lane, 2) == 0
    row_even = even[:1]

    def twice(w):
        return jnp.concatenate([w, w], axis=1)

    def put_left(ref, rows, w, lanes=0):
        hi, lo = parts(w)
        both = jnp.where(low_half, hi.astype(F32), lo.astype(F32)).astype(BF16)
        ref[rows, lanes:lanes + L] = both
        ref[rows, lanes + L:lanes + 2 * L] = both

    def block(i):
        return slice(i * D, (i + 1) * D)

    for i in (2, 3, 4):
        loads[i].wait()
    m_hi, m_lo = parts(twice(m_raw[...]))
    m_both = jnp.where(low_half, m_hi.astype(F32), m_lo.astype(F32)).astype(BF16)
    m_left = jnp.concatenate([m_both, m_both], axis=1)
    order = ((XLO, 0), (XHI, 1), (YLO, 2), (YHI, 3), (ZLO, 4), (ZHI, 5))
    raw = {CEN: twice(s_raw[...])}
    for blk, face in order:
        raw[blk] = twice(f_raw[face])
    stacked = jnp.concatenate([raw[blk] for blk in range(7)], axis=1)
    folded = dot(m_left, split_rows(stacked))
    eye = (lax.rem(lane, D) == lax.broadcasted_iota(jnp.int32, (D, L), 0)).astype(F32)
    for blk in range(7):
        w = folded[:, col(blk)]
        put_left(gst, block(blk), eye - w if blk == CEN else w)

    loads[5].wait()
    k8 = k_raw[...]
    inv8 = 1.0 / k8
    for c in range(8):
        krow[c // 4, 0:1, col(c % 4)] = k8[c:c + 1]
        krow[c // 4, 1:2, col(c % 4)] = inv8[c:c + 1]
        rhs[c // 4, :, col(c % 4)] = b_raw[pl.ds(c, D, stride=8), :]
    for x in range(2):
        const[x] = dot(m_left, split_rows(rhs[x])) * krow[x, 1:2, :]

    def weigh(ke, kn):
        return jnp.where(kn > 0, 2.0 * kn / (ke + kn), 0.0)

    def weight(blk, c):
        return alpha[blk, c:c + 1, :]

    for blk in range(7):
        put_left(rst, block(blk), -raw[blk] if blk == CEN else raw[blk])
    loads[6].wait()
    twins, doubled = [], []
    for abc in range(8):
        w = twice(p_raw[abc])
        doubled.append(w)
        put_left(pst, block(abc), w)
        hi, lo = parts(w)
        right_form = jnp.concatenate([hi, lo], axis=1)
        twins += [right_form, right_form]
    for ref, i, blk, chosen in ((gpx, 0, XLO, (4, 5, 6, 7)), (gpx, 1, XHI, (0, 1, 2, 3)),
                                (gpy, 0, YLO, (2, 3, 6, 7)), (gpy, 1, YHI, (0, 1, 4, 5))):
        both = dot(gst[block(blk), :], split_rows(jnp.concatenate([doubled[abc] for abc in chosen], axis=1)))
        for n in range(4):
            put_left(ref.at[i], block(n), both[:, col(n)])
    folded_p = lax.dot_general(m_left, jnp.concatenate(twins, axis=0), (((1,), (1,)), ((), ())),
                               preferred_element_type=F32)
    for abc in range(8):
        ab, c = divmod(abc, 2)
        put_left(qst, block(c), folded_p[:, col(abc)], 2 * L * ab)

    arrive(*kcopies)
    row8 = lax.broadcasted_iota(jnp.int32, (8, L), 0)
    lane8 = lax.broadcasted_iota(jnp.int32, (8, L), 1)
    y8 = lax.rem(row8, 4)
    kylo, kyhi, kxlo, kxhi = (hk[i] for i in range(4))
    neighbours = {
        XLO: jnp.where(row8 < 4, roll(kxlo, 4, 0), roll(k8, 4, 0)),
        XHI: jnp.where(row8 < 4, roll(k8, 4, 0), roll(kxhi, 4, 0)),
        YLO: jnp.where(y8 == 0, roll(kylo, -3, 0), roll(k8, 1, 0)),
        YHI: jnp.where(y8 == 3, roll(kyhi, 3, 0), roll(k8, -1, 0)),
        ZLO: jnp.where(lane8 == 0, 0.0, roll(k8, 1)),
        ZHI: jnp.where(lane8 == L - 1, 0.0, roll(k8, -1)),
    }
    for blk, kn in neighbours.items():
        alpha[blk] = weigh(k8, kn)

    def coarse_k(k):
        def one(q):
            s = (k[2 * q:2 * q + 1] + k[2 * q + 1:2 * q + 2]) + (k[4 + 2 * q:5 + 2 * q] + k[5 + 2 * q:6 + 2 * q])
            return (s + roll(s, -1)) * 0.125

        return jnp.where(row_even, one(0), roll(one(1), 1))

    kc = coarse_k(k8)
    lane1 = lax.broadcasted_iota(jnp.int32, (1, L), 1)
    cylo, cyhi = coarse_k(kylo), coarse_k(kyhi)
    coarse_neighbours = {
        XLO: coarse_k(kxlo),
        XHI: coarse_k(kxhi),
        YLO: jnp.where(row_even, roll(cylo, -1), roll(kc, 1)),
        YHI: jnp.where(row_even, roll(kc, -1), roll(cyhi, 1)),
        ZLO: jnp.where(lane1 < 2, 0.0, roll(kc, 2)),
        ZHI: jnp.where(lane1 >= L - 2, 0.0, roll(kc, -2)),
    }
    for blk, kn in coarse_neighbours.items():
        calpha[blk:blk + 1, :] = weigh(kc, kn)
    inv_kc = 1.0 / kc

    ends_first = (0, 4, 3, 7, 1, 5, 2, 6)

    def own_part(target, v, stack, base, scale, prod, wide, ends_done=None):
        for x in range(2):
            rows = slice(0, 7 * D) if wide else slice(x * D, (6 + x) * D)
            prod[x, rows, :] = dot(stack[rows, :], split_rows(v[x]))
        for c in ends_first:
            x, y = divmod(c, 4)

            def term(blk, x, y):
                return prod[x, block(blk), col(y)]

            acc = term(CEN, x, y)
            acc += weight(ZLO, c) * roll(term(ZLO, x, y), 1)
            acc += weight(ZHI, c) * roll(term(ZHI, x, y), -1)
            if x == 0:
                acc += weight(XHI, c) * term(XHI, 1, y)
            else:
                acc += weight(XLO, c) * term(XLO, 0, y)
            if y > 0:
                acc += weight(YLO, c) * term(YLO, x, y - 1)
            if y < 3:
                acc += weight(YHI, c) * term(YHI, x, y + 1)
            if scale is not None:
                acc = acc * scale[x, 0:1, col(y)]
            target[x, :, col(y)] = base[x, :, col(y)] + acc
            if c == 7 and ends_done is not None:
                ends_done()

    def halo_products(stack, hx, hy, copies=()):
        found = []
        for i in range(2):
            arrive(*copies[2 + i:3 + i])
            found.append(dot(stack[block((XLO, XHI)[i]), :], split_rows(hx[i])))
        for j in range(2):
            arrive(*copies[j:j + 1])
            found.append(dot(stack[block((YLO, YHI)[j]), :],
                             split_rows(jnp.concatenate([hy[j, 0], hy[j, 1]], axis=1))))
        return found

    def halo_part(target, part, products, scale, ends_done=None):
        from_xlo, from_xhi, from_ylo, from_yhi = products
        for c in ends_first:
            x, y = divmod(c, 4)
            acc = weight(XLO, c) * from_xlo[:, col(y)] if x == 0 else weight(XHI, c) * from_xhi[:, col(y)]
            if y == 0:
                acc += weight(YLO, c) * from_ylo[:, col(x)]
            if y == 3:
                acc += weight(YHI, c) * from_yhi[:, col(x)]
            if scale is not None:
                acc = acc * scale[x, 0:1, col(y)]
            value = part[x, :, col(y)] + acc
            if target is out:
                out[pl.ds(c, D, stride=8), :] = value
            else:
                target[x, :, col(y)] = value
            if c == 7 and ends_done is not None:
                ends_done()

    def complete_halo(hx, hy, hpx, hpy, edge, copies):
        arrive(*copies)

        def edges(i, j):
            return split_rows(jnp.concatenate([edge[i], edge[j]], axis=1))

        from_edge = {XLO: dot(gst[block(XLO), :], edges(0, 1)), XHI: dot(gst[block(XHI), :], edges(2, 3)),
                     YLO: dot(gst[block(YLO), :], edges(0, 2)), YHI: dot(gst[block(YHI), :], edges(1, 3))}
        kx, ky = (kxlo, kxhi), (kylo, kyhi)
        for i in range(2):
            mine, theirs = ((XLO, XHI), (XHI, XLO))[i]
            for y in range(4):
                c = 4 * i + y
                value = hpx[i, :, col(y)] + (2.0 - weight(mine, c)) * prod1[i, block(theirs), col(y)]
                if y in (0, 3):
                    j = y // 3
                    w = weigh(kx[i][4 * (1 - i) + y:4 * (1 - i) + y + 1],
                              hkc[2 * i + j][4 * (1 - i) + 3 - y:4 * (1 - i) + 4 - y])
                    value += w * from_edge[(YLO, YHI)[j]][:, col(i)]
                hx[i, :, col(y)] = value
        for j in range(2):
            mine, theirs = ((YLO, YHI), (YHI, YLO))[j]
            y = 3 * j
            for x in range(2):
                value = hpy[j, x] + (2.0 - weight(mine, 4 * x + y)) * prod1[x, block(theirs), col(y)]
                e, n = 4 * x + 3 - y, 4 * (1 - x) + 3 - y
                w = weigh(ky[j][e:e + 1], hkc[2 * x + j][n:n + 1])
                value += w * from_edge[(XLO, XHI)[x]][:, col(j)]
                hy[j, x] = value

    later = []
    own_part(part0, v0, gst, const, None, prod, False)

    def ends_of_v1():
        later.extend(send_y(v1, hy1) + send_edges(v1, edge1))

    halo_part(v1, part0, halo_products(gst, hx0, hy0, first), None, ends_of_v1)
    second, edges1 = later[:2], later[2:]
    second = second + send_x(v1, hx1)
    parts1 = [send(k_raw, hkc.at[(1 - dx) + (1 - dy) // 2], (dx, dy)) for dx, dy in diagonals]
    own_part(part1, v1, gst, const, None, prod1, True, lambda: parts1.extend(send_y(part1, hpy1)))
    parts1 += send_x(part1, hpx1)
    halo_part(v2, part1, halo_products(gst, hx1, hy1, second), None)

    own_part(part2, v2, rst, rhs, krow, prod, False)
    complete_halo(hx2, hy2, hpx1, hpy1, edge1, edges1 + parts1)
    halo_part(res, part2, halo_products(rst, hx2, hy2), krow)
    r_right = [split_rows(res[x]) for x in range(2)]
    columns = []
    for a in range(2):
        for b in range(2):
            columns.append(jnp.concatenate([r_right[a][:, col(b)], r_right[a][:, col(2 + b)]], axis=1))
    t = dot(qst[...], jnp.concatenate(columns, axis=0))
    packed = jnp.where(even, t[:D, :L] + roll(t[D:, :L], -1), roll(t[:D, L:], 1) + t[D:, L:])
    c1[...] = packed * inv_kc

    third = send_tile(c1, hc1)
    for i, product in enumerate(halo_products(gst, hx2, hy2)):
        if i < 2:
            ghx[i] = product
        else:
            ghy[i - 2] = product
    corr1 = c1[...]
    y = dot(gst[D:4 * D, :], split_rows(corr1))
    acc = corr1 + y[:D]
    acc += calpha[ZLO:ZLO + 1, :] * roll(y[D:2 * D], 2)
    acc += calpha[ZHI:ZHI + 1, :] * roll(y[2 * D:], -2)
    arrive(third[2])
    acc += calpha[XLO:XLO + 1, :] * dot(gst[block(XLO), :], split_rows(hc1[2]))
    arrive(third[3])
    acc += calpha[XHI:XHI + 1, :] * dot(gst[block(XHI), :], split_rows(hc1[3]))
    arrive(third[0])
    below = jnp.where(even, roll(hc1[0], -1), roll(corr1, 1))
    acc += calpha[YLO:YLO + 1, :] * dot(gst[block(YLO), :], split_rows(below))
    arrive(third[1])
    above = jnp.where(even, roll(corr1, -1), roll(hc1[1], 1))
    acc += calpha[YHI:YHI + 1, :] * dot(gst[block(YHI), :], split_rows(above))
    c2[...] = acc

    fourth = send_tile(c2, hc2)

    def lift(o, q):
        if q == 0:
            return jnp.where(even, o[:D], roll(o[D:], 1))
        return jnp.where(even, roll(o[:D], -1), o[D:])

    def pair(o, i):
        return o[2 * i * D:2 * (i + 1) * D]

    o = dot(pst[...], split_rows(c2[...]))
    for c in range(8):
        x, y = divmod(c, 4)
        q, b = divmod(y, 2)
        lifted[x, :, col(y)] = v2[x, :, col(y)] + lift(pair(o, 2 * x + b), q)
    parts3 = send_edges(lifted, edge3)
    own_part(part3, lifted, gst, const, None, prod1, True, lambda: parts3.extend(send_y(part3, hpy3)))
    parts3 += send_x(part3, hpx3)
    products = []
    for i in range(2):
        arrive(fourth[2 + i])
        o = dot(gpx[i], split_rows(hc2[2 + i]))
        products.append(ghx[i] + jnp.concatenate([lift(pair(o, y % 2), y // 2) for y in range(4)], axis=1))
    for j in range(2):
        arrive(fourth[j])
        o = dot(gpy[j], split_rows(hc2[j]))
        products.append(ghy[j] + jnp.concatenate([lift(pair(o, x), 1 - j) for x in range(2)], axis=1))
    halo_part(v3, part3, products, None)
    own_part(part0, v3, gst, const, None, prod, False)
    complete_halo(hx3, hy3, hpx3, hpy3, edge3, parts3)
    halo_part(out, part0, halo_products(gst, hx3, hy3), None)
    for copy, d in sent:
        pl.when(has[d])(copy.wait_send)


def on_device(nx, ny, start_field, right_side, coefficient, stiffness, smoother, face_coupling, prolongation):
    flat = lambda x: x.reshape(8 * D, L)
    field = pltpu.VMEM((2, D, 4 * L), F32)
    small = pltpu.VMEM((D, L), F32)
    four = pltpu.VMEM((4, D, L), F32)
    kfour = pltpu.VMEM((4, 8, L), F32)
    xhalo = pltpu.VMEM((2, D, 4 * L), F32)
    yhalo = pltpu.VMEM((2, 2, D, L), F32)
    sends = 40

    def body(*refs):
        kernel(nx, ny, *refs)

    result = pl.pallas_call(
        body,
        out_shape=jax.ShapeDtypeStruct((8 * D, L), F32),
        in_specs=[pl.BlockSpec(memory_space=pltpu.HBM)] * 7,
        out_specs=pl.BlockSpec(memory_space=pltpu.VMEM),
        scratch_shapes=[
            pltpu.VMEM((8 * D, L), F32), pltpu.VMEM((8 * D, L), F32), pltpu.VMEM((8, L), F32),
            pltpu.VMEM((D, D), F32), pltpu.VMEM((D, D), F32), pltpu.VMEM((6, D, D), F32), pltpu.VMEM((8, D, D), F32),
            *[field] * 12, pltpu.VMEM((2, 7 * D, 4 * L), F32), pltpu.VMEM((2, 7 * D, 4 * L), F32),
            *[xhalo, yhalo] * 6, four, four, kfour, kfour, small, small, four, four,
            pltpu.VMEM((7 * D, 4 * D), BF16), pltpu.VMEM((7 * D, 4 * D), BF16),
            pltpu.VMEM((8 * D, 4 * D), BF16), pltpu.VMEM((2 * D, 16 * D), BF16),
            pltpu.VMEM((2, 4 * D, 4 * D), BF16), pltpu.VMEM((2, 4 * D, 4 * D), BF16), xhalo, pltpu.VMEM((2, D, 2 * L), F32),
            pltpu.VMEM((7, 8, L), F32), pltpu.VMEM((8, L), F32), pltpu.VMEM((2, 8, 4 * L), F32),
            pltpu.SemaphoreType.DMA((7,)), pltpu.SemaphoreType.DMA((sends,)), pltpu.SemaphoreType.DMA((sends,)),
        ],
        compiler_params=pltpu.CompilerParams(
            collective_id=0, has_side_effects=True, vmem_limit_bytes=40 * 2**20),
    )(*(pltpu.with_memory_space_constraint(x, pltpu.HBM) for x in (
        flat(start_field), flat(right_side), coefficient.reshape(8, L), stiffness, smoother, face_coupling,
        prolongation.reshape(8, D, D))))
    return result.reshape(start_field.shape)


def solution(mesh):
    nx, ny = mesh.shape["gx"], mesh.shape["gy"]
    placed = (P(None, "gx", "gy", None), P(None, "gx", "gy", None), P("gx", "gy", None), P(), P(), P(), P())

    def run(*args):
        return on_device(nx, ny, *args)

    return jax.shard_map(
        run, mesh=mesh, in_specs=placed, out_specs=P(None, "gx", "gy", None), check_vma=False)
```

```python
import jax
import jax.numpy as jnp
from jax import lax
from jax.experimental import pallas as pl
from jax.experimental.pallas import tpu as pltpu
from jax.sharding import PartitionSpec as P

MESH = pl.DeviceIdType.MESH
F32 = jnp.float32
BF16 = jnp.bfloat16
D = 64
L = 128
XLO, CEN, ZLO, ZHI, YLO, YHI, XHI = range(7)


def parts(x):
    hi = x.astype(BF16)
    lo = (x - hi.astype(F32)).astype(BF16)
    return hi, lo


def split_rows(x):
    hi, lo = parts(x)
    return jnp.concatenate([hi, hi, lo, lo], axis=0)


def dot(a, b):
    return jnp.dot(a, b, preferred_element_type=F32)


def roll(x, shift, axis=1):
    return pltpu.roll(x, shift % x.shape[axis], axis)


def col(c):
    return slice(c * L, (c + 1) * L)


def kernel(nx, ny, v_in, b_in, k_in, s_in, m_in, f_in, p_in, out,
           v_raw, b_raw, k_raw, s_raw, m_raw, f_raw, p_raw,
           v0, v1, v2, v3, rhs, const, res, lifted, part0, part1, part2, part3, prod, prod1,
           hx0, hy0, hx1, hy1, hpx1, hpy1, hx2, hy2, hpx3, hpy3, hx3, hy3, edge1, edge3, corner2, corner_c2, hk, hkc, c1, c2, hc1, hc2,
           gst, rst, pst, qst, gpx, gpy, ghx, ghy, alpha, calpha, krow, local_sem, send_sem, recv_sem):
    gx, gy = lax.axis_index("gx"), lax.axis_index("gy")
    has = {(-1, 0): gx > 0, (1, 0): gx < nx - 1, (0, -1): gy > 0, (0, 1): gy < ny - 1}
    for dx in (-1, 1):
        for dy in (-1, 1):
            has[dx, dy] = jnp.logical_and(has[dx, 0], has[0, dy])
    faces = ((0, -1), (0, 1), (-1, 0), (1, 0))
    diagonals = ((-1, -1), (-1, 1), (1, -1), (1, 1))
    odd = lax.rem(gx, 2)
    away_x = gx + 2 * odd - 1
    has_away = jnp.logical_and(away_x >= 0, away_x < nx)

    loads = [pltpu.make_async_copy(src, dst, local_sem.at[i]) for i, (src, dst) in enumerate(
        ((k_in, k_raw), (v_in, v_raw), (m_in, m_raw), (s_in, s_raw), (f_in, f_raw), (b_in, b_raw), (p_in, p_raw)))]
    barrier = pltpu.get_barrier_semaphore()
    for d in faces:
        @pl.when(has[d])
        def _(d=d):
            pl.semaphore_signal(barrier, inc=1, device_id=(gx + d[0], gy + d[1]), device_id_type=MESH)
    for load in loads[:2]:
        load.start()

    sent = []

    def put(src, dst, device, out_if, in_if):
        slot = len(sent)
        copy = pltpu.make_async_remote_copy(
            src_ref=src, dst_ref=dst, send_sem=send_sem.at[slot], recv_sem=recv_sem.at[slot],
            device_id=device, device_id_type=MESH)
        pl.when(out_if)(copy.start)
        sent.append((copy, out_if))
        return copy, in_if

    def send(src, dst, d):
        return put(src, dst, (gx + d[0], gy + d[1]), has[d], has[-d[0], -d[1]])

    def relay(src, dst, j):
        there = has[0, 2 * j - 1]
        return put(src, dst, (gx + 1 - 2 * odd, gy), there, there)

    def arrive(*copies):
        for copy, in_if in copies:
            pl.when(in_if)(copy.wait_recv)

    def send_y(v, hy):
        return [send(v.at[:, :, col(3)], hy.at[0], (0, 1)), send(v.at[:, :, col(0)], hy.at[1], (0, -1))]

    def send_x(v, hx):
        return [send(v.at[1], hx.at[0], (1, 0)), send(v.at[0], hx.at[1], (-1, 0))]

    def send_edges(v, edge):
        return [put(v.at[odd, :, col(3 if dy > 0 else 0)], edge.at[2 * (1 - odd) + (1 - dy) // 2], (away_x, gy + dy),
                    jnp.logical_and(has_away, has[0, dy]), jnp.logical_and(has_away, has[0, -dy])) for dy in (-1, 1)]

    def send_tile(c, h):
        return (send(c, h.at[0], (0, 1)), send(c, h.at[1], (0, -1)), send(c, h.at[2], (1, 0)), send(c, h.at[3], (-1, 0)))

    loads[1].wait()
    for load in loads[2:]:
        load.start()
    for c in range(8):
        v0[c // 4, :, col(c % 4)] = v_raw[pl.ds(c, D, stride=8), :]
    loads[0].wait()
    count = has[-1, 0].astype(jnp.int32) + has[1, 0].astype(jnp.int32) + has[0, -1].astype(jnp.int32) + has[0, 1].astype(jnp.int32)
    pl.semaphore_wait(barrier, count)
    kcopies = send_tile(k_raw, hk)
    first = send_y(v0, hy0) + send_x(v0, hx0)

    for d, y_at, x_at in (((0, -1), 0, None), ((0, 1), 1, None), ((-1, 0), None, 0), ((1, 0), None, 1)):
        @pl.when(jnp.logical_not(has[d]))
        def _(y_at=y_at, x_at=x_at):
            if x_at is None:
                for ref in (hy0, hy1, hpy1, hpy3):
                    ref[y_at] = jnp.zeros_like(ref[y_at])
                for ref in (hk, hc1, hc2):
                    ref[y_at] = jnp.zeros_like(ref[y_at])
                for i in range(2):
                    for ref in (edge1, edge3, corner2, corner_c2, hkc):
                        ref[2 * i + y_at] = jnp.zeros_like(ref[0])
            else:
                for ref in (hx0, hx1, hpx1, hpx3):
                    ref[x_at] = jnp.zeros_like(ref[x_at])
                for ref in (hk, hc1, hc2):
                    ref[2 + x_at] = jnp.zeros_like(ref[0])
                for j in range(2):
                    for ref in (edge1, edge3, corner2, corner_c2, hkc):
                        ref[2 * x_at + j] = jnp.zeros_like(ref[0])

    lane = lax.broadcasted_iota(jnp.int32, (D, L), 1)
    low_half = lane < D
    even = lax.rem(lane, 2) == 0
    row_even = even[:1]

    def twice(w):
        return jnp.concatenate([w, w], axis=1)

    def put_left(ref, rows, w, lanes=0):
        hi, lo = parts(w)
        both = jnp.where(low_half, hi.astype(F32), lo.astype(F32)).astype(BF16)
        ref[rows, lanes:lanes + L] = both
        ref[rows, lanes + L:lanes + 2 * L] = both

    def block(i):
        return slice(i * D, (i + 1) * D)

    for i in (2, 3, 4):
        loads[i].wait()
    m_hi, m_lo = parts(twice(m_raw[...]))
    m_both = jnp.where(low_half, m_hi.astype(F32), m_lo.astype(F32)).astype(BF16)
    m_left = jnp.concatenate([m_both, m_both], axis=1)
    order = ((XLO, 0), (XHI, 1), (YLO, 2), (YHI, 3), (ZLO, 4), (ZHI, 5))
    raw = {CEN: twice(s_raw[...])}
    for blk, face in order:
        raw[blk] = twice(f_raw[face])
    stacked = jnp.concatenate([raw[blk] for blk in range(7)], axis=1)
    folded = dot(m_left, split_rows(stacked))
    eye = (lax.rem(lane, D) == lax.broadcasted_iota(jnp.int32, (D, L), 0)).astype(F32)
    for blk in range(7):
        w = folded[:, col(blk)]
        put_left(gst, block(blk), eye - w if blk == CEN else w)

    loads[5].wait()
    k8 = k_raw[...]
    inv8 = 1.0 / k8
    for c in range(8):
        krow[c // 4, 0:1, col(c % 4)] = k8[c:c + 1]
        krow[c // 4, 1:2, col(c % 4)] = inv8[c:c + 1]
        rhs[c // 4, :, col(c % 4)] = b_raw[pl.ds(c, D, stride=8), :]
    for x in range(2):
        const[x] = dot(m_left, split_rows(rhs[x])) * krow[x, 1:2, :]

    def weigh(ke, kn):
        return jnp.where(kn > 0, 2.0 * kn / (ke + kn), 0.0)

    def weight(blk, c):
        return alpha[blk, c:c + 1, :]

    for blk in range(7):
        put_left(rst, block(blk), -raw[blk] if blk == CEN else raw[blk])
    loads[6].wait()
    twins, doubled = [], []
    for abc in range(8):
        w = twice(p_raw[abc])
        doubled.append(w)
        put_left(pst, block(abc), w)
        hi, lo = parts(w)
        right_form = jnp.concatenate([hi, lo], axis=1)
        twins += [right_form, right_form]
    for ref, i, blk, chosen in ((gpx, 0, XLO, (4, 5, 6, 7)), (gpx, 1, XHI, (0, 1, 2, 3)),
                                (gpy, 0, YLO, (2, 3, 6, 7)), (gpy, 1, YHI, (0, 1, 4, 5))):
        both = dot(gst[block(blk), :], split_rows(jnp.concatenate([doubled[abc] for abc in chosen], axis=1)))
        for n in range(4):
            put_left(ref.at[i], block(n), both[:, col(n)])
    folded_p = lax.dot_general(m_left, jnp.concatenate(twins, axis=0), (((1,), (1,)), ((), ())),
                               preferred_element_type=F32)
    for abc in range(8):
        ab, c = divmod(abc, 2)
        put_left(qst, block(c), folded_p[:, col(abc)], 2 * L * ab)

    arrive(*kcopies)
    row8 = lax.broadcasted_iota(jnp.int32, (8, L), 0)
    lane8 = lax.broadcasted_iota(jnp.int32, (8, L), 1)
    y8 = lax.rem(row8, 4)
    kylo, kyhi, kxlo, kxhi = (hk[i] for i in range(4))
    neighbours = {
        XLO: jnp.where(row8 < 4, roll(kxlo, 4, 0), roll(k8, 4, 0)),
        XHI: jnp.where(row8 < 4, roll(k8, 4, 0), roll(kxhi, 4, 0)),
        YLO: jnp.where(y8 == 0, roll(kylo, -3, 0), roll(k8, 1, 0)),
        YHI: jnp.where(y8 == 3, roll(kyhi, 3, 0), roll(k8, -1, 0)),
        ZLO: jnp.where(lane8 == 0, 0.0, roll(k8, 1)),
        ZHI: jnp.where(lane8 == L - 1, 0.0, roll(k8, -1)),
    }
    for blk, kn in neighbours.items():
        alpha[blk] = weigh(k8, kn)

    def coarse_k(k):
        def one(q):
            s = (k[2 * q:2 * q + 1] + k[2 * q + 1:2 * q + 2]) + (k[4 + 2 * q:5 + 2 * q] + k[5 + 2 * q:6 + 2 * q])
            return (s + roll(s, -1)) * 0.125

        return jnp.where(row_even, one(0), roll(one(1), 1))

    kc = coarse_k(k8)
    lane1 = lax.broadcasted_iota(jnp.int32, (1, L), 1)
    cylo, cyhi = coarse_k(kylo), coarse_k(kyhi)
    coarse_neighbours = {
        XLO: coarse_k(kxlo),
        XHI: coarse_k(kxhi),
        YLO: jnp.where(row_even, roll(cylo, -1), roll(kc, 1)),
        YHI: jnp.where(row_even, roll(kc, -1), roll(cyhi, 1)),
        ZLO: jnp.where(lane1 < 2, 0.0, roll(kc, 2)),
        ZHI: jnp.where(lane1 >= L - 2, 0.0, roll(kc, -2)),
    }
    for blk, kn in coarse_neighbours.items():
        calpha[blk:blk + 1, :] = weigh(kc, kn)
    inv_kc = 1.0 / kc

    ends_first = (0, 4, 3, 7, 1, 5, 2, 6)

    def own_part(target, v, stack, base, scale, prod, wide, ends_done=None):
        for x in range(2):
            rows = slice(0, 7 * D) if wide else slice(x * D, (6 + x) * D)
            prod[x, rows, :] = dot(stack[rows, :], split_rows(v[x]))
        for c in ends_first:
            x, y = divmod(c, 4)

            def term(blk, x, y):
                return prod[x, block(blk), col(y)]

            acc = term(CEN, x, y)
            acc += weight(ZLO, c) * roll(term(ZLO, x, y), 1)
            acc += weight(ZHI, c) * roll(term(ZHI, x, y), -1)
            if x == 0:
                acc += weight(XHI, c) * term(XHI, 1, y)
            else:
                acc += weight(XLO, c) * term(XLO, 0, y)
            if y > 0:
                acc += weight(YLO, c) * term(YLO, x, y - 1)
            if y < 3:
                acc += weight(YHI, c) * term(YHI, x, y + 1)
            if scale is not None:
                acc = acc * scale[x, 0:1, col(y)]
            target[x, :, col(y)] = base[x, :, col(y)] + acc
            if c == 7 and ends_done is not None:
                ends_done()

    def halo_products(stack, hx, hy, copies=(), passed_on=None):
        found_x, found_y = [], []
        arrive(*copies)
        for j in range(2):
            if passed_on is not None:
                passed_on(j)
        for j in range(2):
            found_y.append(dot(stack[block((YLO, YHI)[j]), :],
                               split_rows(jnp.concatenate([hy[j, 0], hy[j, 1]], axis=1))))
        for i in range(2):
            found_x.append(dot(stack[block((XLO, XHI)[i]), :], split_rows(hx[i])))
        return found_x + found_y

    def halo_part(target, part, products, scale, ends_done=None):
        from_xlo, from_xhi, from_ylo, from_yhi = products
        for c in ends_first:
            x, y = divmod(c, 4)
            acc = weight(XLO, c) * from_xlo[:, col(y)] if x == 0 else weight(XHI, c) * from_xhi[:, col(y)]
            if y == 0:
                acc += weight(YLO, c) * from_ylo[:, col(x)]
            if y == 3:
                acc += weight(YHI, c) * from_yhi[:, col(x)]
            if scale is not None:
                acc = acc * scale[x, 0:1, col(y)]
            value = part[x, :, col(y)] + acc
            if target is out:
                out[pl.ds(c, D, stride=8), :] = value
            else:
                target[x, :, col(y)] = value
            if c == 7 and ends_done is not None:
                ends_done()

    def complete_halo(hx, hy, hpx, hpy, edge, copies):
        arrive(*copies)

        def edges(i, j):
            return split_rows(jnp.concatenate([edge[i], edge[j]], axis=1))

        from_edge = {XLO: dot(gst[block(XLO), :], edges(0, 1)), XHI: dot(gst[block(XHI), :], edges(2, 3)),
                     YLO: dot(gst[block(YLO), :], edges(0, 2)), YHI: dot(gst[block(YHI), :], edges(1, 3))}
        kx, ky = (kxlo, kxhi), (kylo, kyhi)
        for i in range(2):
            mine, theirs = ((XLO, XHI), (XHI, XLO))[i]
            for y in range(4):
                c = 4 * i + y
                value = hpx[i, :, col(y)] + (2.0 - weight(mine, c)) * prod1[i, block(theirs), col(y)]
                if y in (0, 3):
                    j = y // 3
                    w = weigh(kx[i][4 * (1 - i) + y:4 * (1 - i) + y + 1],
                              hkc[2 * i + j][4 * (1 - i) + 3 - y:4 * (1 - i) + 4 - y])
                    value += w * from_edge[(YLO, YHI)[j]][:, col(i)]
                hx[i, :, col(y)] = value
        for j in range(2):
            mine, theirs = ((YLO, YHI), (YHI, YLO))[j]
            y = 3 * j
            for x in range(2):
                value = hpy[j, x] + (2.0 - weight(mine, 4 * x + y)) * prod1[x, block(theirs), col(y)]
                e, n = 4 * x + 3 - y, 4 * (1 - x) + 3 - y
                w = weigh(ky[j][e:e + 1], hkc[2 * x + j][n:n + 1])
                value += w * from_edge[(XLO, XHI)[x]][:, col(j)]
                hy[j, x] = value

    later = []
    own_part(part0, v0, gst, const, None, prod, False)

    def ends_of_v1():
        later.extend(send_y(v1, hy1) + send_edges(v1, edge1))

    halo_part(v1, part0, halo_products(gst, hx0, hy0, first), None, ends_of_v1)
    second, edges1 = later[:2], later[2:]
    second = second + send_x(v1, hx1)
    parts1 = [send(k_raw, hkc.at[(1 - dx) + (1 - dy) // 2], (dx, dy)) for dx, dy in diagonals]
    own_part(part1, v1, gst, const, None, prod1, True, lambda: parts1.extend(send_y(part1, hpy1)))
    parts1 += send_x(part1, hpx1)
    halo_part(v2, part1, halo_products(gst, hx1, hy1, second, lambda j: parts1.append(
        relay(hy1.at[j, 1 - odd], edge1.at[2 * odd + j], j))), None)

    own_part(part2, v2, rst, rhs, krow, prod, False)
    complete_halo(hx2, hy2, hpx1, hpy1, edge1, edges1 + parts1)
    corners2 = [relay(hy2.at[j, 1 - odd], corner2.at[2 * odd + j], j) for j in range(2)]
    halo_part(res, part2, halo_products(rst, hx2, hy2), krow)
    r_right = [split_rows(res[x]) for x in range(2)]
    columns = []
    for a in range(2):
        for b in range(2):
            columns.append(jnp.concatenate([r_right[a][:, col(b)], r_right[a][:, col(2 + b)]], axis=1))
    t = dot(qst[...], jnp.concatenate(columns, axis=0))
    packed = jnp.where(even, t[:D, :L] + roll(t[D:, :L], -1), roll(t[:D, L:], 1) + t[D:, L:])
    c1[...] = packed * inv_kc

    third = send_tile(c1, hc1)
    for i, product in enumerate(halo_products(gst, hx2, hy2)):
        if i < 2:
            ghx[i] = product
        else:
            ghy[i - 2] = product
    corr1 = c1[...]
    y = dot(gst[D:4 * D, :], split_rows(corr1))
    acc = corr1 + y[:D]
    acc += calpha[ZLO:ZLO + 1, :] * roll(y[D:2 * D], 2)
    acc += calpha[ZHI:ZHI + 1, :] * roll(y[2 * D:], -2)
    arrive(*third)
    acc += calpha[XLO:XLO + 1, :] * dot(gst[block(XLO), :], split_rows(hc1[2]))
    acc += calpha[XHI:XHI + 1, :] * dot(gst[block(XHI), :], split_rows(hc1[3]))
    below = jnp.where(even, roll(hc1[0], -1), roll(corr1, 1))
    acc += calpha[YLO:YLO + 1, :] * dot(gst[block(YLO), :], split_rows(below))
    above = jnp.where(even, roll(corr1, -1), roll(hc1[1], 1))
    acc += calpha[YHI:YHI + 1, :] * dot(gst[block(YHI), :], split_rows(above))
    c2[...] = acc

    fourth = send_tile(c2, hc2)

    def lift(o, q):
        if q == 0:
            return jnp.where(even, o[:D], roll(o[D:], 1))
        return jnp.where(even, roll(o[:D], -1), o[D:])

    def pair(o, i):
        return o[2 * i * D:2 * (i + 1) * D]

    o = dot(pst[...], split_rows(c2[...]))
    for c in range(8):
        x, y = divmod(c, 4)
        q, b = divmod(y, 2)
        lifted[x, :, col(y)] = v2[x, :, col(y)] + lift(pair(o, 2 * x + b), q)
    parts3 = send_edges(lifted, edge3)
    own_part(part3, lifted, gst, const, None, prod1, True, lambda: parts3.extend(send_y(part3, hpy3)))
    parts3 += send_x(part3, hpx3)
    products = []
    passed = []
    arrive(*fourth)
    for j in range(2):
        passed.append(relay(hc2.at[j], corner_c2.at[2 * odd + j], j))
    for j in range(2):
        o = dot(gpy[j], split_rows(hc2[j]))
        products.append(ghy[j] + jnp.concatenate([lift(pair(o, x), 1 - j) for x in range(2)], axis=1))
    for i in range(2):
        o = dot(gpx[i], split_rows(hc2[2 + i]))
        products.insert(i, ghx[i] + jnp.concatenate([lift(pair(o, y % 2), y // 2) for y in range(4)], axis=1))
    halo_part(v3, part3, products, None)
    arrive(*corners2, *passed)
    for j in range(2):
        at = 2 * (1 - odd) + j
        rows = pl.ds(pl.multiple_of(odd * 4 * D + (1 - j) * L, L), L)
        edge3[at] = corner2[at] + lift(dot(pst[rows, :], split_rows(corner_c2[at])), 1 - j)
    own_part(part0, v3, gst, const, None, prod, False)
    complete_halo(hx3, hy3, hpx3, hpy3, edge3, parts3)
    halo_part(out, part0, halo_products(gst, hx3, hy3), None)
    for copy, out_if in sent:
        pl.when(out_if)(copy.wait_send)


def on_device(nx, ny, start_field, right_side, coefficient, stiffness, smoother, face_coupling, prolongation):
    flat = lambda x: x.reshape(8 * D, L)
    field = pltpu.VMEM((2, D, 4 * L), F32)
    small = pltpu.VMEM((D, L), F32)
    four = pltpu.VMEM((4, D, L), F32)
    kfour = pltpu.VMEM((4, 8, L), F32)
    xhalo = pltpu.VMEM((2, D, 4 * L), F32)
    yhalo = pltpu.VMEM((2, 2, D, L), F32)
    sends = 42

    def body(*refs):
        kernel(nx, ny, *refs)

    result = pl.pallas_call(
        body,
        out_shape=jax.ShapeDtypeStruct((8 * D, L), F32),
        in_specs=[pl.BlockSpec(memory_space=pltpu.HBM)] * 7,
        out_specs=pl.BlockSpec(memory_space=pltpu.VMEM),
        scratch_shapes=[
            pltpu.VMEM((8 * D, L), F32), pltpu.VMEM((8 * D, L), F32), pltpu.VMEM((8, L), F32),
            pltpu.VMEM((D, D), F32), pltpu.VMEM((D, D), F32), pltpu.VMEM((6, D, D), F32), pltpu.VMEM((8, D, D), F32),
            *[field] * 12, pltpu.VMEM((2, 7 * D, 4 * L), F32), pltpu.VMEM((2, 7 * D, 4 * L), F32),
            *[xhalo, yhalo] * 6, four, four, four, four, kfour, kfour, small, small, four, four,
            pltpu.VMEM((7 * D, 4 * D), BF16), pltpu.VMEM((7 * D, 4 * D), BF16),
            pltpu.VMEM((8 * D, 4 * D), BF16), pltpu.VMEM((2 * D, 16 * D), BF16),
            pltpu.VMEM((2, 4 * D, 4 * D), BF16), pltpu.VMEM((2, 4 * D, 4 * D), BF16), xhalo, pltpu.VMEM((2, D, 2 * L), F32),
            pltpu.VMEM((7, 8, L), F32), pltpu.VMEM((8, L), F32), pltpu.VMEM((2, 8, 4 * L), F32),
            pltpu.SemaphoreType.DMA((7,)), pltpu.SemaphoreType.DMA((sends,)), pltpu.SemaphoreType.DMA((sends,)),
        ],
        compiler_params=pltpu.CompilerParams(
            collective_id=0, has_side_effects=True, vmem_limit_bytes=40 * 2**20),
    )(*(pltpu.with_memory_space_constraint(x, pltpu.HBM) for x in (
        flat(start_field), flat(right_side), coefficient.reshape(8, L), stiffness, smoother, face_coupling,
        prolongation.reshape(8, D, D))))
    return result.reshape(start_field.shape)


def solution(mesh):
    nx, ny = mesh.shape["gx"], mesh.shape["gy"]
    placed = (P(None, "gx", "gy", None), P(None, "gx", "gy", None), P("gx", "gy", None), P(), P(), P(), P())

    def run(*args):
        return on_device(nx, ny, *args)

    return jax.shard_map(
        run, mesh=mesh, in_specs=placed, out_specs=P(None, "gx", "gy", None), check_vma=False)
```

```python
import jax
import jax.numpy as jnp
from jax import lax
from jax.experimental import pallas as pl
from jax.experimental.pallas import tpu as pltpu
from jax.sharding import PartitionSpec as P

MESH = pl.DeviceIdType.MESH
F32 = jnp.float32
BF16 = jnp.bfloat16
D = 64
L = 128
XLO, CEN, ZLO, ZHI, YLO, YHI, XHI = range(7)


def parts(x):
    hi = x.astype(BF16)
    lo = (x - hi.astype(F32)).astype(BF16)
    return hi, lo


def split_rows(x):
    hi, lo = parts(x)
    return jnp.concatenate([hi, hi, lo, lo], axis=0)


def dot(a, b):
    return jnp.dot(a, b, preferred_element_type=F32)


def roll(x, shift, axis=1):
    return pltpu.roll(x, shift % x.shape[axis], axis)


def col(c):
    return slice(c * L, (c + 1) * L)


def kernel(nx, ny, v_in, b_in, k_in, s_in, m_in, f_in, p_in, out,
           v_raw, b_raw, k_raw, s_raw, m_raw, f_raw, p_raw,
           v0, v1, v2, v3, rhs, const, res, lifted, part0, part1, part2, part3, prod, prod1,
           hx0, hy0, hx1, hy1, hpx1, hpy1, hx2, hy2, hpx3, hpy3, hx3, hy3, edge1, edge3, corner2, corner_c2, hk, hkc, c1, c2, hc1, hc2,
           gst, rst, pst, qst, gpx, gpy, ghx, ghy, alpha, calpha, krow, local_sem, send_sem, recv_sem):
    gx, gy = lax.axis_index("gx"), lax.axis_index("gy")
    has = {(-1, 0): gx > 0, (1, 0): gx < nx - 1, (0, -1): gy > 0, (0, 1): gy < ny - 1}
    for dx in (-1, 1):
        for dy in (-1, 1):
            has[dx, dy] = jnp.logical_and(has[dx, 0], has[0, dy])
    faces = ((0, -1), (0, 1), (-1, 0), (1, 0))
    diagonals = ((-1, -1), (-1, 1), (1, -1), (1, 1))
    odd = lax.rem(gx, 2)
    away_x = gx + 2 * odd - 1
    has_away = jnp.logical_and(away_x >= 0, away_x < nx)

    loads = [pltpu.make_async_copy(src, dst, local_sem.at[i]) for i, (src, dst) in enumerate(
        ((k_in, k_raw), (v_in, v_raw), (m_in, m_raw), (s_in, s_raw), (f_in, f_raw), (b_in, b_raw), (p_in, p_raw)))]
    barrier = pltpu.get_barrier_semaphore()
    for d in faces:
        @pl.when(has[d])
        def _(d=d):
            pl.semaphore_signal(barrier, inc=1, device_id=(gx + d[0], gy + d[1]), device_id_type=MESH)
    for load in loads[:2]:
        load.start()

    sent = []

    def put(src, dst, device, out_if, in_if):
        slot = len(sent)
        copy = pltpu.make_async_remote_copy(
            src_ref=src, dst_ref=dst, send_sem=send_sem.at[slot], recv_sem=recv_sem.at[slot],
            device_id=device, device_id_type=MESH)
        pl.when(out_if)(copy.start)
        sent.append((copy, out_if))
        return copy, in_if

    def send(src, dst, d):
        return put(src, dst, (gx + d[0], gy + d[1]), has[d], has[-d[0], -d[1]])

    def relay(src, dst, j):
        there = has[0, 2 * j - 1]
        return put(src, dst, (gx + 1 - 2 * odd, gy), there, there)

    def arrive(*copies):
        for copy, in_if in copies:
            pl.when(in_if)(copy.wait_recv)

    def send_y(v, hy):
        return [send(v.at[:, :, col(3)], hy.at[0], (0, 1)), send(v.at[:, :, col(0)], hy.at[1], (0, -1))]

    def send_x(v, hx):
        return [send(v.at[1], hx.at[0], (1, 0)), send(v.at[0], hx.at[1], (-1, 0))]

    def send_edges(v, edge):
        return [put(v.at[odd, :, col(3 if dy > 0 else 0)], edge.at[2 * (1 - odd) + (1 - dy) // 2], (away_x, gy + dy),
                    jnp.logical_and(has_away, has[0, dy]), jnp.logical_and(has_away, has[0, -dy])) for dy in (-1, 1)]

    def send_tile(c, h):
        return (send(c, h.at[0], (0, 1)), send(c, h.at[1], (0, -1)), send(c, h.at[2], (1, 0)), send(c, h.at[3], (-1, 0)))

    loads[1].wait()
    for load in loads[2:]:
        load.start()
    for c in range(8):
        v0[c // 4, :, col(c % 4)] = v_raw[pl.ds(c, D, stride=8), :]
    loads[0].wait()
    count = has[-1, 0].astype(jnp.int32) + has[1, 0].astype(jnp.int32) + has[0, -1].astype(jnp.int32) + has[0, 1].astype(jnp.int32)
    pl.semaphore_wait(barrier, count)
    kcopies = send_tile(k_raw, hk)
    first = send_y(v0, hy0) + send_x(v0, hx0)

    for d, y_at, x_at in (((0, -1), 0, None), ((0, 1), 1, None), ((-1, 0), None, 0), ((1, 0), None, 1)):
        @pl.when(jnp.logical_not(has[d]))
        def _(y_at=y_at, x_at=x_at):
            if x_at is None:
                for ref in (hy0, hy1, hpy1, hpy3):
                    ref[y_at] = jnp.zeros_like(ref[y_at])
                for ref in (hk, hc1, hc2):
                    ref[y_at] = jnp.zeros_like(ref[y_at])
                for i in range(2):
                    for ref in (edge1, edge3, corner2, corner_c2, hkc):
                        ref[2 * i + y_at] = jnp.zeros_like(ref[0])
            else:
                for ref in (hx0, hx1, hpx1, hpx3):
                    ref[x_at] = jnp.zeros_like(ref[x_at])
                for ref in (hk, hc1, hc2):
                    ref[2 + x_at] = jnp.zeros_like(ref[0])
                for j in range(2):
                    for ref in (edge1, edge3, corner2, corner_c2, hkc):
                        ref[2 * x_at + j] = jnp.zeros_like(ref[0])

    lane = lax.broadcasted_iota(jnp.int32, (D, L), 1)
    low_half = lane < D
    even = lax.rem(lane, 2) == 0
    row_even = even[:1]

    def twice(w):
        return jnp.concatenate([w, w], axis=1)

    def put_left(ref, rows, w, lanes=0):
        hi, lo = parts(w)
        both = jnp.where(low_half, hi.astype(F32), lo.astype(F32)).astype(BF16)
        ref[rows, lanes:lanes + L] = both
        ref[rows, lanes + L:lanes + 2 * L] = both

    def block(i):
        return slice(i * D, (i + 1) * D)

    for i in (2, 3, 4):
        loads[i].wait()
    m_hi, m_lo = parts(twice(m_raw[...]))
    m_both = jnp.where(low_half, m_hi.astype(F32), m_lo.astype(F32)).astype(BF16)
    m_left = jnp.concatenate([m_both, m_both], axis=1)
    order = ((XLO, 0), (XHI, 1), (YLO, 2), (YHI, 3), (ZLO, 4), (ZHI, 5))
    raw = {CEN: twice(s_raw[...])}
    for blk, face in order:
        raw[blk] = twice(f_raw[face])
    stacked = jnp.concatenate([raw[blk] for blk in range(7)], axis=1)
    folded = dot(m_left, split_rows(stacked))
    eye = (lax.rem(lane, D) == lax.broadcasted_iota(jnp.int32, (D, L), 0)).astype(F32)
    for blk in range(7):
        w = folded[:, col(blk)]
        put_left(gst, block(blk), eye - w if blk == CEN else w)

    loads[5].wait()
    k8 = k_raw[...]
    inv8 = 1.0 / k8
    for c in range(8):
        krow[c // 4, 0:1, col(c % 4)] = k8[c:c + 1]
        krow[c // 4, 1:2, col(c % 4)] = inv8[c:c + 1]
        rhs[c // 4, :, col(c % 4)] = b_raw[pl.ds(c, D, stride=8), :]
    for x in range(2):
        const[x] = dot(m_left, split_rows(rhs[x])) * krow[x, 1:2, :]

    def weigh(ke, kn):
        return jnp.where(kn > 0, 2.0 * kn / (ke + kn), 0.0)

    def weight(blk, c):
        return alpha[blk, c:c + 1, :]

    for blk in range(7):
        put_left(rst, block(blk), -raw[blk] if blk == CEN else raw[blk])
    loads[6].wait()
    twins, doubled = [], []
    for abc in range(8):
        w = twice(p_raw[abc])
        doubled.append(w)
        put_left(pst, block(abc), w)
        hi, lo = parts(w)
        right_form = jnp.concatenate([hi, lo], axis=1)
        twins += [right_form, right_form]
    for ref, i, blk, chosen in ((gpx, 0, XLO, (4, 5, 6, 7)), (gpx, 1, XHI, (0, 1, 2, 3)),
                                (gpy, 0, YLO, (2, 3, 6, 7)), (gpy, 1, YHI, (0, 1, 4, 5))):
        both = dot(gst[block(blk), :], split_rows(jnp.concatenate([doubled[abc] for abc in chosen], axis=1)))
        for n in range(4):
            put_left(ref.at[i], block(n), both[:, col(n)])
    folded_p = lax.dot_general(m_left, jnp.concatenate(twins, axis=0), (((1,), (1,)), ((), ())),
                               preferred_element_type=F32)
    for abc in range(8):
        ab, c = divmod(abc, 2)
        put_left(qst, block(c), folded_p[:, col(abc)], 2 * L * ab)

    row8 = lax.broadcasted_iota(jnp.int32, (8, L), 0)
    lane8 = lax.broadcasted_iota(jnp.int32, (8, L), 1)
    y8 = lax.rem(row8, 4)
    own_neighbours = {
        XLO: roll(k8, 4, 0),
        XHI: roll(k8, 4, 0),
        YLO: roll(k8, 1, 0),
        YHI: roll(k8, -1, 0),
        ZLO: jnp.where(lane8 == 0, 0.0, roll(k8, 1)),
        ZHI: jnp.where(lane8 == L - 1, 0.0, roll(k8, -1)),
    }
    for blk, kn in own_neighbours.items():
        alpha[blk] = weigh(k8, kn)

    ends_first = (0, 4, 3, 7, 1, 5, 2, 6)

    def own_part(target, v, stack, base, scale, prod, wide, ends_done=None):
        for x in range(2):
            rows = slice(0, 7 * D) if wide else slice(x * D, (6 + x) * D)
            prod[x, rows, :] = dot(stack[rows, :], split_rows(v[x]))
        for c in ends_first:
            x, y = divmod(c, 4)

            def term(blk, x, y):
                return prod[x, block(blk), col(y)]

            acc = term(CEN, x, y)
            acc += weight(ZLO, c) * roll(term(ZLO, x, y), 1)
            acc += weight(ZHI, c) * roll(term(ZHI, x, y), -1)
            if x == 0:
                acc += weight(XHI, c) * term(XHI, 1, y)
            else:
                acc += weight(XLO, c) * term(XLO, 0, y)
            if y > 0:
                acc += weight(YLO, c) * term(YLO, x, y - 1)
            if y < 3:
                acc += weight(YHI, c) * term(YHI, x, y + 1)
            if scale is not None:
                acc = acc * scale[x, 0:1, col(y)]
            target[x, :, col(y)] = base[x, :, col(y)] + acc
            if c == 7 and ends_done is not None:
                ends_done()

    def halo_products(stack, hx, hy, copies=(), passed_on=None):
        found_x, found_y = [], []
        arrive(*copies[:2])
        for j in range(2):
            if passed_on is not None:
                passed_on(j)
        arrive(*copies[2:])
        for j in range(2):
            found_y.append(dot(stack[block((YLO, YHI)[j]), :],
                               split_rows(jnp.concatenate([hy[j, 0], hy[j, 1]], axis=1))))
        for i in range(2):
            found_x.append(dot(stack[block((XLO, XHI)[i]), :], split_rows(hx[i])))
        return found_x + found_y

    def halo_part(target, part, products, scale, ends_done=None):
        from_xlo, from_xhi, from_ylo, from_yhi = products
        for c in ends_first:
            x, y = divmod(c, 4)
            acc = weight(XLO, c) * from_xlo[:, col(y)] if x == 0 else weight(XHI, c) * from_xhi[:, col(y)]
            if y == 0:
                acc += weight(YLO, c) * from_ylo[:, col(x)]
            if y == 3:
                acc += weight(YHI, c) * from_yhi[:, col(x)]
            if scale is not None:
                acc = acc * scale[x, 0:1, col(y)]
            value = part[x, :, col(y)] + acc
            if target is out:
                out[pl.ds(c, D, stride=8), :] = value
            else:
                target[x, :, col(y)] = value
            if c == 7 and ends_done is not None:
                ends_done()

    def complete_halo(hx, hy, hpx, hpy, edge, copies):
        arrive(*copies)

        def edges(i, j):
            return split_rows(jnp.concatenate([edge[i], edge[j]], axis=1))

        from_edge = {XLO: dot(gst[block(XLO), :], edges(0, 1)), XHI: dot(gst[block(XHI), :], edges(2, 3)),
                     YLO: dot(gst[block(YLO), :], edges(0, 2)), YHI: dot(gst[block(YHI), :], edges(1, 3))}
        kx, ky = (kxlo, kxhi), (kylo, kyhi)
        for i in range(2):
            mine, theirs = ((XLO, XHI), (XHI, XLO))[i]
            for y in range(4):
                c = 4 * i + y
                value = hpx[i, :, col(y)] + (2.0 - weight(mine, c)) * prod1[i, block(theirs), col(y)]
                if y in (0, 3):
                    j = y // 3
                    w = weigh(kx[i][4 * (1 - i) + y:4 * (1 - i) + y + 1],
                              hkc[2 * i + j][4 * (1 - i) + 3 - y:4 * (1 - i) + 4 - y])
                    value += w * from_edge[(YLO, YHI)[j]][:, col(i)]
                hx[i, :, col(y)] = value
        for j in range(2):
            mine, theirs = ((YLO, YHI), (YHI, YLO))[j]
            y = 3 * j
            for x in range(2):
                value = hpy[j, x] + (2.0 - weight(mine, 4 * x + y)) * prod1[x, block(theirs), col(y)]
                e, n = 4 * x + 3 - y, 4 * (1 - x) + 3 - y
                w = weigh(ky[j][e:e + 1], hkc[2 * x + j][n:n + 1])
                value += w * from_edge[(XLO, XHI)[x]][:, col(j)]
                hy[j, x] = value

    later = []
    own_part(part0, v0, gst, const, None, prod, False)
    arrive(*kcopies)
    kylo, kyhi, kxlo, kxhi = (hk[i] for i in range(4))
    neighbours = {
        XLO: jnp.where(row8 < 4, roll(kxlo, 4, 0), own_neighbours[XLO]),
        XHI: jnp.where(row8 < 4, own_neighbours[XHI], roll(kxhi, 4, 0)),
        YLO: jnp.where(y8 == 0, roll(kylo, -3, 0), own_neighbours[YLO]),
        YHI: jnp.where(y8 == 3, roll(kyhi, 3, 0), own_neighbours[YHI]),
    }
    for blk, kn in neighbours.items():
        alpha[blk] = weigh(k8, kn)


    def ends_of_v1():
        later.extend(send_edges(v1, edge1) + send_y(v1, hy1))

    halo_part(v1, part0, halo_products(gst, hx0, hy0, first), None, ends_of_v1)
    edges1, second = later[:2], later[2:]
    second = second + send_x(v1, hx1)
    parts1 = [send(k_raw, hkc.at[(1 - dx) + (1 - dy) // 2], (dx, dy)) for dx, dy in diagonals]
    own_part(part1, v1, gst, const, None, prod1, True, lambda: parts1.extend(send_y(part1, hpy1)))
    parts1 += send_x(part1, hpx1)

    def coarse_k(k):
        def one(q):
            s = (k[2 * q:2 * q + 1] + k[2 * q + 1:2 * q + 2]) + (k[4 + 2 * q:5 + 2 * q] + k[5 + 2 * q:6 + 2 * q])
            return (s + roll(s, -1)) * 0.125

        return jnp.where(row_even, one(0), roll(one(1), 1))

    kc = coarse_k(k8)
    lane1 = lax.broadcasted_iota(jnp.int32, (1, L), 1)
    cylo, cyhi = coarse_k(kylo), coarse_k(kyhi)
    coarse_neighbours = {
        XLO: coarse_k(kxlo),
        XHI: coarse_k(kxhi),
        YLO: jnp.where(row_even, roll(cylo, -1), roll(kc, 1)),
        YHI: jnp.where(row_even, roll(kc, -1), roll(cyhi, 1)),
        ZLO: jnp.where(lane1 < 2, 0.0, roll(kc, 2)),
        ZHI: jnp.where(lane1 >= L - 2, 0.0, roll(kc, -2)),
    }
    for blk, kn in coarse_neighbours.items():
        calpha[blk:blk + 1, :] = weigh(kc, kn)
    inv_kc = 1.0 / kc

    halo_part(v2, part1, halo_products(gst, hx1, hy1, second, lambda j: parts1.append(
        relay(hy1.at[j, 1 - odd], edge1.at[2 * odd + j], j))), None)

    own_part(part2, v2, rst, rhs, krow, prod, False)
    complete_halo(hx2, hy2, hpx1, hpy1, edge1, edges1 + parts1)
    halo_part(res, part2, halo_products(rst, hx2, hy2), krow)
    r_right = [split_rows(res[x]) for x in range(2)]
    columns = []
    for a in range(2):
        for b in range(2):
            columns.append(jnp.concatenate([r_right[a][:, col(b)], r_right[a][:, col(2 + b)]], axis=1))
    t = dot(qst[...], jnp.concatenate(columns, axis=0))
    packed = jnp.where(even, t[:D, :L] + roll(t[D:, :L], -1), roll(t[:D, L:], 1) + t[D:, L:])
    c1[...] = packed * inv_kc

    third = send_tile(c1, hc1)
    corners2 = [relay(hy2.at[j, 1 - odd], corner2.at[2 * odd + j], j) for j in range(2)]
    for i, product in enumerate(halo_products(gst, hx2, hy2)):
        if i < 2:
            ghx[i] = product
        else:
            ghy[i - 2] = product
    corr1 = c1[...]
    y = dot(gst[D:4 * D, :], split_rows(corr1))
    acc = corr1 + y[:D]
    acc += calpha[ZLO:ZLO + 1, :] * roll(y[D:2 * D], 2)
    acc += calpha[ZHI:ZHI + 1, :] * roll(y[2 * D:], -2)
    arrive(*third)
    acc += calpha[XLO:XLO + 1, :] * dot(gst[block(XLO), :], split_rows(hc1[2]))
    acc += calpha[XHI:XHI + 1, :] * dot(gst[block(XHI), :], split_rows(hc1[3]))
    below = jnp.where(even, roll(hc1[0], -1), roll(corr1, 1))
    acc += calpha[YLO:YLO + 1, :] * dot(gst[block(YLO), :], split_rows(below))
    above = jnp.where(even, roll(corr1, -1), roll(hc1[1], 1))
    acc += calpha[YHI:YHI + 1, :] * dot(gst[block(YHI), :], split_rows(above))
    c2[...] = acc

    fourth = send_tile(c2, hc2)

    def lift(o, q):
        if q == 0:
            return jnp.where(even, o[:D], roll(o[D:], 1))
        return jnp.where(even, roll(o[:D], -1), o[D:])

    def pair(o, i):
        return o[2 * i * D:2 * (i + 1) * D]

    o = dot(pst[...], split_rows(c2[...]))
    for c in range(8):
        x, y = divmod(c, 4)
        q, b = divmod(y, 2)
        lifted[x, :, col(y)] = v2[x, :, col(y)] + lift(pair(o, 2 * x + b), q)
    parts3 = send_edges(lifted, edge3)
    own_part(part3, lifted, gst, const, None, prod1, True, lambda: parts3.extend(send_y(part3, hpy3)))
    parts3 += send_x(part3, hpx3)
    products = []
    passed = []
    arrive(*fourth[:2])
    for j in range(2):
        passed.append(relay(hc2.at[j], corner_c2.at[2 * odd + j], j))
    arrive(*fourth[2:])
    for j in range(2):
        o = dot(gpy[j], split_rows(hc2[j]))
        products.append(ghy[j] + jnp.concatenate([lift(pair(o, x), 1 - j) for x in range(2)], axis=1))
    for i in range(2):
        o = dot(gpx[i], split_rows(hc2[2 + i]))
        products.insert(i, ghx[i] + jnp.concatenate([lift(pair(o, y % 2), y // 2) for y in range(4)], axis=1))
    halo_part(v3, part3, products, None)
    own_part(part0, v3, gst, const, None, prod, False)
    arrive(*corners2, *passed)
    for j in range(2):
        at = 2 * (1 - odd) + j
        rows = pl.ds(pl.multiple_of(odd * 4 * D + (1 - j) * L, L), L)
        edge3[at] = corner2[at] + lift(dot(pst[rows, :], split_rows(corner_c2[at])), 1 - j)
    complete_halo(hx3, hy3, hpx3, hpy3, edge3, parts3)
    halo_part(out, part0, halo_products(gst, hx3, hy3), None)
    for copy, out_if in sent:
        pl.when(out_if)(copy.wait_send)


def on_device(nx, ny, start_field, right_side, coefficient, stiffness, smoother, face_coupling, prolongation):
    flat = lambda x: x.reshape(8 * D, L)
    field = pltpu.VMEM((2, D, 4 * L), F32)
    small = pltpu.VMEM((D, L), F32)
    four = pltpu.VMEM((4, D, L), F32)
    kfour = pltpu.VMEM((4, 8, L), F32)
    xhalo = pltpu.VMEM((2, D, 4 * L), F32)
    yhalo = pltpu.VMEM((2, 2, D, L), F32)
    sends = 42

    def body(*refs):
        kernel(nx, ny, *refs)

    result = pl.pallas_call(
        body,
        out_shape=jax.ShapeDtypeStruct((8 * D, L), F32),
        in_specs=[pl.BlockSpec(memory_space=pltpu.HBM)] * 7,
        out_specs=pl.BlockSpec(memory_space=pltpu.VMEM),
        scratch_shapes=[
            pltpu.VMEM((8 * D, L), F32), pltpu.VMEM((8 * D, L), F32), pltpu.VMEM((8, L), F32),
            pltpu.VMEM((D, D), F32), pltpu.VMEM((D, D), F32), pltpu.VMEM((6, D, D), F32), pltpu.VMEM((8, D, D), F32),
            *[field] * 12, pltpu.VMEM((2, 7 * D, 4 * L), F32), pltpu.VMEM((2, 7 * D, 4 * L), F32),
            *[xhalo, yhalo] * 6, four, four, four, four, kfour, kfour, small, small, four, four,
            pltpu.VMEM((7 * D, 4 * D), BF16), pltpu.VMEM((7 * D, 4 * D), BF16),
            pltpu.VMEM((8 * D, 4 * D), BF16), pltpu.VMEM((2 * D, 16 * D), BF16),
            pltpu.VMEM((2, 4 * D, 4 * D), BF16), pltpu.VMEM((2, 4 * D, 4 * D), BF16), xhalo, pltpu.VMEM((2, D, 2 * L), F32),
            pltpu.VMEM((7, 8, L), F32), pltpu.VMEM((8, L), F32), pltpu.VMEM((2, 8, 4 * L), F32),
            pltpu.SemaphoreType.DMA((7,)), pltpu.SemaphoreType.DMA((sends,)), pltpu.SemaphoreType.DMA((sends,)),
        ],
        compiler_params=pltpu.CompilerParams(
            collective_id=0, has_side_effects=True, vmem_limit_bytes=40 * 2**20),
    )(*(pltpu.with_memory_space_constraint(x, pltpu.HBM) for x in (
        flat(start_field), flat(right_side), coefficient.reshape(8, L), stiffness, smoother, face_coupling,
        prolongation.reshape(8, D, D))))
    return result.reshape(start_field.shape)


def solution(mesh):
    nx, ny = mesh.shape["gx"], mesh.shape["gy"]
    placed = (P(None, "gx", "gy", None), P(None, "gx", "gy", None), P("gx", "gy", None), P(), P(), P(), P())

    def run(*args):
        return on_device(nx, ny, *args)

    return jax.shard_map(
        run, mesh=mesh, in_specs=placed, out_specs=P(None, "gx", "gy", None), check_vma=False)
```

```python
import jax
import jax.numpy as jnp
from jax import lax
from jax.experimental import pallas as pl
from jax.experimental.pallas import tpu as pltpu
from jax.sharding import PartitionSpec as P

MESH = pl.DeviceIdType.MESH
F32 = jnp.float32
BF16 = jnp.bfloat16
D = 64
L = 128
XLO, CEN, ZLO, ZHI, YLO, YHI, XHI = range(7)


def parts(x):
    hi = x.astype(BF16)
    lo = (x - hi.astype(F32)).astype(BF16)
    return hi, lo


def split_rows(x):
    hi, lo = parts(x)
    return jnp.concatenate([hi, hi, lo], axis=0)


def dot(a, b):
    return jnp.dot(a[:, :b.shape[0]], b, preferred_element_type=F32)


def roll(x, shift, axis=1):
    return pltpu.roll(x, shift % x.shape[axis], axis)


def col(c):
    return slice(c * L, (c + 1) * L)


def kernel(nx, ny, v_in, b_in, k_in, s_in, m_in, f_in, p_in, part0, out_x, out_y, alpha,
           v_raw, b_raw, k_raw, s_raw, m_raw, f_raw, p_raw,
           v0, v1, v2, v3, rhs, const, res, lifted, part1, part2, part3, prod, prod1,
           hx0, hy0, hx1, hy1, hpx1, hpy1, hx2, hy2, hpx3, hpy3, hx3, hy3, edge1, edge3, corner2, corner_c2, hk, hkc, c1, c2, hc1, hc2,
           gst, rst, pst, qst, gpx, gpy, ghx, ghy, calpha, krow, local_sem, send_sem, recv_sem):
    gx, gy = lax.axis_index("gx"), lax.axis_index("gy")
    has = {(-1, 0): gx > 0, (1, 0): gx < nx - 1, (0, -1): gy > 0, (0, 1): gy < ny - 1}
    for dx in (-1, 1):
        for dy in (-1, 1):
            has[dx, dy] = jnp.logical_and(has[dx, 0], has[0, dy])
    faces = ((0, -1), (0, 1), (-1, 0), (1, 0))
    diagonals = ((-1, -1), (-1, 1), (1, -1), (1, 1))
    odd = lax.rem(gx, 2)
    away_x = gx + 2 * odd - 1
    has_away = jnp.logical_and(away_x >= 0, away_x < nx)

    loads = [pltpu.make_async_copy(src, dst, local_sem.at[i]) for i, (src, dst) in enumerate(
        ((k_in, k_raw), (v_in, v_raw), (m_in, m_raw), (s_in, s_raw), (f_in, f_raw), (b_in, b_raw), (p_in, p_raw)))]
    barrier = pltpu.get_barrier_semaphore()
    for d in faces:
        @pl.when(has[d])
        def _(d=d):
            pl.semaphore_signal(barrier, inc=1, device_id=(gx + d[0], gy + d[1]), device_id_type=MESH)
    for load in loads[:2]:
        load.start()

    sent = []

    def put(src, dst, device, out_if, in_if):
        slot = len(sent)
        copy = pltpu.make_async_remote_copy(
            src_ref=src, dst_ref=dst, send_sem=send_sem.at[slot], recv_sem=recv_sem.at[slot],
            device_id=device, device_id_type=MESH)
        pl.when(out_if)(copy.start)
        sent.append((copy, out_if))
        return copy, in_if

    def send(src, dst, d):
        return put(src, dst, (gx + d[0], gy + d[1]), has[d], has[-d[0], -d[1]])

    def relay(src, dst, j):
        there = has[0, 2 * j - 1]
        return put(src, dst, (gx + 1 - 2 * odd, gy), there, there)

    def arrive(*copies):
        for copy, in_if in copies:
            pl.when(in_if)(copy.wait_recv)

    def send_y(v, hy):
        return [send(v.at[:, :, col(3)], hy.at[0], (0, 1)), send(v.at[:, :, col(0)], hy.at[1], (0, -1))]

    def send_x(v, hx):
        return [send(v.at[1], hx.at[0], (1, 0)), send(v.at[0], hx.at[1], (-1, 0))]

    def send_edges(v, edge):
        return [put(v.at[odd, :, col(3 if dy > 0 else 0)], edge.at[2 * (1 - odd) + (1 - dy) // 2], (away_x, gy + dy),
                    jnp.logical_and(has_away, has[0, dy]), jnp.logical_and(has_away, has[0, -dy])) for dy in (-1, 1)]

    def send_tile(c, h):
        return (send(c, h.at[0], (0, 1)), send(c, h.at[1], (0, -1)), send(c, h.at[2], (1, 0)), send(c, h.at[3], (-1, 0)))

    loads[1].wait()
    for load in loads[2:]:
        load.start()
    for c in range(8):
        v0[c // 4, :, col(c % 4)] = v_raw[pl.ds(c, D, stride=8), :]
    loads[0].wait()
    count = has[-1, 0].astype(jnp.int32) + has[1, 0].astype(jnp.int32) + has[0, -1].astype(jnp.int32) + has[0, 1].astype(jnp.int32)
    pl.semaphore_wait(barrier, count)
    kcopies = send_tile(k_raw, hk)
    first = send_y(v0, hy0) + send_x(v0, hx0)

    for d, y_at, x_at in (((0, -1), 0, None), ((0, 1), 1, None), ((-1, 0), None, 0), ((1, 0), None, 1)):
        @pl.when(jnp.logical_not(has[d]))
        def _(y_at=y_at, x_at=x_at):
            if x_at is None:
                for ref in (hy0, hy1, hpy1, hpy3):
                    ref[y_at] = jnp.zeros_like(ref[y_at])
                for ref in (hk, hc1, hc2):
                    ref[y_at] = jnp.zeros_like(ref[y_at])
                for i in range(2):
                    for ref in (edge1, edge3, corner2, corner_c2, hkc):
                        ref[2 * i + y_at] = jnp.zeros_like(ref[0])
            else:
                for ref in (hx0, hx1, hpx1, hpx3):
                    ref[x_at] = jnp.zeros_like(ref[x_at])
                for ref in (hk, hc1, hc2):
                    ref[2 + x_at] = jnp.zeros_like(ref[0])
                for j in range(2):
                    for ref in (edge1, edge3, corner2, corner_c2, hkc):
                        ref[2 * x_at + j] = jnp.zeros_like(ref[0])

    lane = lax.broadcasted_iota(jnp.int32, (D, L), 1)
    low_half = lane < D
    even = lax.rem(lane, 2) == 0
    row_even = even[:1]

    def twice(w):
        return jnp.concatenate([w, w], axis=1)

    def put_left(ref, rows, w, lanes=0):
        hi, lo = parts(w)
        both = jnp.where(low_half, hi.astype(F32), lo.astype(F32)).astype(BF16)
        ref[rows, lanes:lanes + L] = both
        ref[rows, lanes + L:lanes + 2 * L] = both

    def block(i):
        return slice(i * D, (i + 1) * D)

    for i in (2, 3, 4):
        loads[i].wait()
    m_hi, m_lo = parts(twice(m_raw[...]))
    m_both = jnp.where(low_half, m_hi.astype(F32), m_lo.astype(F32)).astype(BF16)
    m_left = jnp.concatenate([m_both, m_both], axis=1)
    order = ((XLO, 0), (XHI, 1), (YLO, 2), (YHI, 3), (ZLO, 4), (ZHI, 5))
    raw = {CEN: twice(s_raw[...])}
    for blk, face in order:
        raw[blk] = twice(f_raw[face])
    stacked = jnp.concatenate([raw[blk] for blk in range(7)], axis=1)
    folded = dot(m_left, split_rows(stacked))
    eye = (lax.rem(lane, D) == lax.broadcasted_iota(jnp.int32, (D, L), 0)).astype(F32)
    for blk in range(7):
        w = folded[:, col(blk)]
        put_left(gst, block(blk), eye - w if blk == CEN else w)

    loads[5].wait()
    k8 = k_raw[...]
    inv8 = 1.0 / k8
    for c in range(8):
        krow[c // 4, 0:1, col(c % 4)] = k8[c:c + 1]
        krow[c // 4, 1:2, col(c % 4)] = inv8[c:c + 1]
        rhs[c // 4, :, col(c % 4)] = b_raw[pl.ds(c, D, stride=8), :]
    for x in range(2):
        const[x] = dot(m_left, split_rows(rhs[x])) * krow[x, 1:2, :]

    def weigh(ke, kn):
        return jnp.where(kn > 0, 2.0 * kn / (ke + kn), 0.0)

    def weight(blk, c):
        return alpha[blk, c:c + 1, :]

    for blk in range(7):
        put_left(rst, block(blk), -raw[blk] if blk == CEN else raw[blk])
    loads[6].wait()
    twins, doubled = [], []
    for abc in range(8):
        w = twice(p_raw[abc])
        doubled.append(w)
        put_left(pst, block(abc), w)
        hi, lo = parts(w)
        right_form = jnp.concatenate([hi, lo], axis=1)
        twins += [right_form, right_form]
    for ref, i, blk, chosen in ((gpx, 0, XLO, (4, 5, 6, 7)), (gpx, 1, XHI, (0, 1, 2, 3)),
                                (gpy, 0, YLO, (2, 3, 6, 7)), (gpy, 1, YHI, (0, 1, 4, 5))):
        both = dot(gst[block(blk), :], split_rows(jnp.concatenate([doubled[abc] for abc in chosen], axis=1)))
        for n in range(4):
            put_left(ref.at[i], block(n), both[:, col(n)])
    folded_p = lax.dot_general(m_left, jnp.concatenate(twins, axis=0), (((1,), (1,)), ((), ())),
                               preferred_element_type=F32)
    for abc in range(8):
        ab, c = divmod(abc, 2)
        put_left(qst, block(c), folded_p[:, col(abc)], 2 * L * ab)

    row8 = lax.broadcasted_iota(jnp.int32, (8, L), 0)
    lane8 = lax.broadcasted_iota(jnp.int32, (8, L), 1)
    y8 = lax.rem(row8, 4)
    own_neighbours = {
        XLO: roll(k8, 4, 0),
        XHI: roll(k8, 4, 0),
        YLO: roll(k8, 1, 0),
        YHI: roll(k8, -1, 0),
        ZLO: jnp.where(lane8 == 0, 0.0, roll(k8, 1)),
        ZHI: jnp.where(lane8 == L - 1, 0.0, roll(k8, -1)),
    }
    for blk, kn in own_neighbours.items():
        alpha[blk] = weigh(k8, kn)

    ends_first = (0, 4, 3, 7, 1, 5, 2, 6)

    def own_part(target, v, stack, base, scale, prod, wide, ends_done=None):
        for x in range(2):
            rows = slice(0, 7 * D) if wide else slice(x * D, (6 + x) * D)
            prod[x, rows, :] = dot(stack[rows, :], split_rows(v[x]))
        for c in ends_first:
            x, y = divmod(c, 4)

            def term(blk, x, y):
                return prod[x, block(blk), col(y)]

            acc = term(CEN, x, y)
            acc += weight(ZLO, c) * roll(term(ZLO, x, y), 1)
            acc += weight(ZHI, c) * roll(term(ZHI, x, y), -1)
            if x == 0:
                acc += weight(XHI, c) * term(XHI, 1, y)
            else:
                acc += weight(XLO, c) * term(XLO, 0, y)
            if y > 0:
                acc += weight(YLO, c) * term(YLO, x, y - 1)
            if y < 3:
                acc += weight(YHI, c) * term(YHI, x, y + 1)
            if scale is not None:
                acc = acc * scale[x, 0:1, col(y)]
            target[x, :, col(y)] = base[x, :, col(y)] + acc
            if c == 7 and ends_done is not None:
                ends_done()

    def halo_products(stack, hx, hy, copies=(), passed_on=None):
        found_x, found_y = [], []
        arrive(*copies[:2])
        for j in range(2):
            if passed_on is not None:
                passed_on(j)
        arrive(*copies[2:])
        for j in range(2):
            found_y.append(dot(stack[block((YLO, YHI)[j]), :],
                               split_rows(jnp.concatenate([hy[j, 0], hy[j, 1]], axis=1))))
        for i in range(2):
            found_x.append(dot(stack[block((XLO, XHI)[i]), :], split_rows(hx[i])))
        return found_x + found_y

    def halo_part(target, part, products, scale, ends_done=None):
        from_xlo, from_xhi, from_ylo, from_yhi = products
        for c in ends_first:
            x, y = divmod(c, 4)
            acc = weight(XLO, c) * from_xlo[:, col(y)] if x == 0 else weight(XHI, c) * from_xhi[:, col(y)]
            if y == 0:
                acc += weight(YLO, c) * from_ylo[:, col(x)]
            if y == 3:
                acc += weight(YHI, c) * from_yhi[:, col(x)]
            if scale is not None:
                acc = acc * scale[x, 0:1, col(y)]
            value = part[x, :, col(y)] + acc
            target[x, :, col(y)] = value
            if c == 7 and ends_done is not None:
                ends_done()

    def complete_halo(hx, hy, hpx, hpy, edge, copies):
        arrive(*copies)

        def edges(i, j):
            return split_rows(jnp.concatenate([edge[i], edge[j]], axis=1))

        from_edge = {XLO: dot(gst[block(XLO), :], edges(0, 1)), XHI: dot(gst[block(XHI), :], edges(2, 3)),
                     YLO: dot(gst[block(YLO), :], edges(0, 2)), YHI: dot(gst[block(YHI), :], edges(1, 3))}
        kx, ky = (kxlo, kxhi), (kylo, kyhi)
        for i in range(2):
            mine, theirs = ((XLO, XHI), (XHI, XLO))[i]
            for y in range(4):
                c = 4 * i + y
                value = hpx[i, :, col(y)] + (2.0 - weight(mine, c)) * prod1[i, block(theirs), col(y)]
                if y in (0, 3):
                    j = y // 3
                    w = weigh(kx[i][4 * (1 - i) + y:4 * (1 - i) + y + 1],
                              hkc[2 * i + j][4 * (1 - i) + 3 - y:4 * (1 - i) + 4 - y])
                    value += w * from_edge[(YLO, YHI)[j]][:, col(i)]
                hx[i, :, col(y)] = value
        for j in range(2):
            mine, theirs = ((YLO, YHI), (YHI, YLO))[j]
            y = 3 * j
            for x in range(2):
                value = hpy[j, x] + (2.0 - weight(mine, 4 * x + y)) * prod1[x, block(theirs), col(y)]
                e, n = 4 * x + 3 - y, 4 * (1 - x) + 3 - y
                w = weigh(ky[j][e:e + 1], hkc[2 * x + j][n:n + 1])
                value += w * from_edge[(XLO, XHI)[x]][:, col(j)]
                hy[j, x] = value

    later = []
    own_part(part0, v0, gst, const, None, prod, False)
    arrive(*kcopies)
    kylo, kyhi, kxlo, kxhi = (hk[i] for i in range(4))
    neighbours = {
        XLO: jnp.where(row8 < 4, roll(kxlo, 4, 0), own_neighbours[XLO]),
        XHI: jnp.where(row8 < 4, own_neighbours[XHI], roll(kxhi, 4, 0)),
        YLO: jnp.where(y8 == 0, roll(kylo, -3, 0), own_neighbours[YLO]),
        YHI: jnp.where(y8 == 3, roll(kyhi, 3, 0), own_neighbours[YHI]),
    }
    for blk, kn in neighbours.items():
        alpha[blk] = weigh(k8, kn)


    def ends_of_v1():
        later.extend(send_edges(v1, edge1) + send_y(v1, hy1))

    halo_part(v1, part0, halo_products(gst, hx0, hy0, first), None, ends_of_v1)
    edges1, second = later[:2], later[2:]
    second = second + send_x(v1, hx1)
    parts1 = [send(k_raw, hkc.at[(1 - dx) + (1 - dy) // 2], (dx, dy)) for dx, dy in diagonals]
    own_part(part1, v1, gst, const, None, prod1, True, lambda: parts1.extend(send_y(part1, hpy1)))
    parts1 += send_x(part1, hpx1)

    def coarse_k(k):
        def one(q):
            s = (k[2 * q:2 * q + 1] + k[2 * q + 1:2 * q + 2]) + (k[4 + 2 * q:5 + 2 * q] + k[5 + 2 * q:6 + 2 * q])
            return (s + roll(s, -1)) * 0.125

        return jnp.where(row_even, one(0), roll(one(1), 1))

    kc = coarse_k(k8)
    lane1 = lax.broadcasted_iota(jnp.int32, (1, L), 1)
    cylo, cyhi = coarse_k(kylo), coarse_k(kyhi)
    coarse_neighbours = {
        XLO: coarse_k(kxlo),
        XHI: coarse_k(kxhi),
        YLO: jnp.where(row_even, roll(cylo, -1), roll(kc, 1)),
        YHI: jnp.where(row_even, roll(kc, -1), roll(cyhi, 1)),
        ZLO: jnp.where(lane1 < 2, 0.0, roll(kc, 2)),
        ZHI: jnp.where(lane1 >= L - 2, 0.0, roll(kc, -2)),
    }
    for blk, kn in coarse_neighbours.items():
        calpha[blk:blk + 1, :] = weigh(kc, kn)
    inv_kc = 1.0 / kc

    halo_part(v2, part1, halo_products(gst, hx1, hy1, second, lambda j: parts1.append(
        relay(hy1.at[j, 1 - odd], edge1.at[2 * odd + j], j))), None)

    own_part(part2, v2, rst, rhs, krow, prod, False)
    complete_halo(hx2, hy2, hpx1, hpy1, edge1, edges1 + parts1)
    halo_part(res, part2, halo_products(rst, hx2, hy2), krow)
    r_right = [split_rows(res[x]) for x in range(2)]
    columns = []
    for a in range(2):
        for b in range(2):
            columns.append(jnp.concatenate([r_right[a][:, col(b)], r_right[a][:, col(2 + b)]], axis=1))
    t = sum(dot(qst[:, 4 * D * ab:4 * D * (ab + 1)], columns[ab]) for ab in range(4))
    packed = jnp.where(even, t[:D, :L] + roll(t[D:, :L], -1), roll(t[:D, L:], 1) + t[D:, L:])
    c1[...] = packed * inv_kc

    third = send_tile(c1, hc1)
    corners2 = [relay(hy2.at[j, 1 - odd], corner2.at[2 * odd + j], j) for j in range(2)]
    for i, product in enumerate(halo_products(gst, hx2, hy2)):
        if i < 2:
            ghx[i] = product
        else:
            ghy[i - 2] = product
    corr1 = c1[...]
    y = dot(gst[D:4 * D, :], split_rows(corr1))
    acc = corr1 + y[:D]
    acc += calpha[ZLO:ZLO + 1, :] * roll(y[D:2 * D], 2)
    acc += calpha[ZHI:ZHI + 1, :] * roll(y[2 * D:], -2)
    arrive(*third)
    acc += calpha[XLO:XLO + 1, :] * dot(gst[block(XLO), :], split_rows(hc1[2]))
    acc += calpha[XHI:XHI + 1, :] * dot(gst[block(XHI), :], split_rows(hc1[3]))
    below = jnp.where(even, roll(hc1[0], -1), roll(corr1, 1))
    acc += calpha[YLO:YLO + 1, :] * dot(gst[block(YLO), :], split_rows(below))
    above = jnp.where(even, roll(corr1, -1), roll(hc1[1], 1))
    acc += calpha[YHI:YHI + 1, :] * dot(gst[block(YHI), :], split_rows(above))
    c2[...] = acc

    fourth = send_tile(c2, hc2)

    def lift(o, q):
        if q == 0:
            return jnp.where(even, o[:D], roll(o[D:], 1))
        return jnp.where(even, roll(o[:D], -1), o[D:])

    def pair(o, i):
        return o[2 * i * D:2 * (i + 1) * D]

    o = dot(pst[...], split_rows(c2[...]))
    for c in range(8):
        x, y = divmod(c, 4)
        q, b = divmod(y, 2)
        lifted[x, :, col(y)] = v2[x, :, col(y)] + lift(pair(o, 2 * x + b), q)
    parts3 = send_edges(lifted, edge3)
    own_part(part3, lifted, gst, const, None, prod1, True, lambda: parts3.extend(send_y(part3, hpy3)))
    parts3 += send_x(part3, hpx3)
    products = []
    passed = []
    arrive(*fourth[:2])
    for j in range(2):
        passed.append(relay(hc2.at[j], corner_c2.at[2 * odd + j], j))
    arrive(*fourth[2:])
    for j in range(2):
        o = dot(gpy[j], split_rows(hc2[j]))
        products.append(ghy[j] + jnp.concatenate([lift(pair(o, x), 1 - j) for x in range(2)], axis=1))
    for i in range(2):
        o = dot(gpx[i], split_rows(hc2[2 + i]))
        products.insert(i, ghx[i] + jnp.concatenate([lift(pair(o, y % 2), y // 2) for y in range(4)], axis=1))
    halo_part(v3, part3, products, None)
    own_part(part0, v3, gst, const, None, prod, False)
    arrive(*corners2, *passed)
    for j in range(2):
        at = 2 * (1 - odd) + j
        rows = pl.ds(pl.multiple_of(odd * 4 * D + (1 - j) * L, L), L)
        edge3[at] = corner2[at] + lift(dot(pst[rows, :], split_rows(corner_c2[at])), 1 - j)
    complete_halo(hx3, hy3, hpx3, hpy3, edge3, parts3)
    for i, product in enumerate(halo_products(gst, hx3, hy3)):
        (out_x if i < 2 else out_y)[i % 2] = product
    for copy, out_if in sent:
        pl.when(out_if)(copy.wait_send)


def finish_kernel(part, from_x, from_y, alpha, out, buffer, sem):
    pieces, height = 4, D // 4
    copies = []
    for p in range(pieces):
        rows = slice(p * height, (p + 1) * height)
        for c in range(8):
            x, y = divmod(c, 4)
            value = part[x, rows, col(y)] + alpha[(XLO, XHI)[x], c:c + 1, :] * from_x[x, rows, col(y)]
            if y in (0, 3):
                value += alpha[(YLO, YHI)[y // 3], c:c + 1, :] * from_y[y // 3, rows, col(x)]
            buffer[pl.ds(8 * p * height + c, height, stride=8), :] = value
        done = slice(8 * p * height, 8 * (p + 1) * height)
        copies.append(pltpu.make_async_copy(buffer.at[done], out.at[done], sem.at[p]))
        copies[-1].start()
    for copy in copies:
        copy.wait()


def finish(*arrays):
    return pl.pallas_call(
        finish_kernel,
        out_shape=jax.ShapeDtypeStruct((8 * D, L), F32),
        in_specs=[pl.BlockSpec(memory_space=pltpu.VMEM)] * 4,
        out_specs=pl.BlockSpec(memory_space=pltpu.HBM),
        scratch_shapes=[pltpu.VMEM((8 * D, L), F32), pltpu.SemaphoreType.DMA((4,))],
        compiler_params=pltpu.CompilerParams(vmem_limit_bytes=16 * 2**20),
    )(*arrays)


def on_device(nx, ny, start_field, right_side, coefficient, stiffness, smoother, face_coupling, prolongation):
    flat = lambda x: x.reshape(8 * D, L)
    field = pltpu.VMEM((2, D, 4 * L), F32)
    small = pltpu.VMEM((D, L), F32)
    four = pltpu.VMEM((4, D, L), F32)
    kfour = pltpu.VMEM((4, 8, L), F32)
    xhalo = pltpu.VMEM((2, D, 4 * L), F32)
    yhalo = pltpu.VMEM((2, 2, D, L), F32)
    sends = 42

    def body(*refs):
        kernel(nx, ny, *refs)

    result = pl.pallas_call(
        body,
        out_shape=[jax.ShapeDtypeStruct(shape, F32) for shape in (
            (2, D, 4 * L), (2, D, 4 * L), (2, D, 2 * L), (7, 8, L))],
        in_specs=[pl.BlockSpec(memory_space=pltpu.HBM)] * 7,
        out_specs=[pl.BlockSpec(memory_space=pltpu.VMEM)] * 4,
        scratch_shapes=[
            pltpu.VMEM((8 * D, L), F32), pltpu.VMEM((8 * D, L), F32), pltpu.VMEM((8, L), F32),
            pltpu.VMEM((D, D), F32), pltpu.VMEM((D, D), F32), pltpu.VMEM((6, D, D), F32), pltpu.VMEM((8, D, D), F32),
            *[field] * 11, pltpu.VMEM((2, 7 * D, 4 * L), F32), pltpu.VMEM((2, 7 * D, 4 * L), F32),
            *[xhalo, yhalo] * 6, four, four, four, four, kfour, kfour, small, small, four, four,
            pltpu.VMEM((7 * D, 4 * D), BF16), pltpu.VMEM((7 * D, 4 * D), BF16),
            pltpu.VMEM((8 * D, 4 * D), BF16), pltpu.VMEM((2 * D, 16 * D), BF16),
            pltpu.VMEM((2, 4 * D, 4 * D), BF16), pltpu.VMEM((2, 4 * D, 4 * D), BF16), xhalo, pltpu.VMEM((2, D, 2 * L), F32),
            pltpu.VMEM((8, L), F32), pltpu.VMEM((2, 8, 4 * L), F32),
            pltpu.SemaphoreType.DMA((7,)), pltpu.SemaphoreType.DMA((sends,)), pltpu.SemaphoreType.DMA((sends,)),
        ],
        compiler_params=pltpu.CompilerParams(
            collective_id=0, has_side_effects=True, vmem_limit_bytes=40 * 2**20),
    )(*(pltpu.with_memory_space_constraint(x, pltpu.HBM) for x in (
        flat(start_field), flat(right_side), coefficient.reshape(8, L), stiffness, smoother, face_coupling,
        prolongation.reshape(8, D, D))))
    return finish(*result).reshape(start_field.shape)


def solution(mesh):
    nx, ny = mesh.shape["gx"], mesh.shape["gy"]
    placed = (P(None, "gx", "gy", None), P(None, "gx", "gy", None), P("gx", "gy", None), P(), P(), P(), P())

    def run(*args):
        return on_device(nx, ny, *args)

    return jax.shard_map(
        run, mesh=mesh, in_specs=placed, out_specs=P(None, "gx", "gy", None), check_vma=False)
```

```python
import jax
import jax.numpy as jnp
from jax import lax
from jax.experimental import pallas as pl
from jax.experimental.pallas import tpu as pltpu
from jax.sharding import PartitionSpec as P

MESH = pl.DeviceIdType.MESH
F32 = jnp.float32
BF16 = jnp.bfloat16
D = 64
L = 128
XLO, CEN, ZLO, ZHI, YLO, YHI, XHI = range(7)


def parts(x):
    hi = x.astype(BF16)
    lo = (x - hi.astype(F32)).astype(BF16)
    return hi, lo


def split_rows(x):
    hi, lo = parts(x)
    return jnp.concatenate([hi, hi, lo], axis=0)


def dot(a, b):
    return jnp.dot(a[:, :b.shape[0]], b, preferred_element_type=F32)


def roll(x, shift, axis=1):
    return pltpu.roll(x, shift % x.shape[axis], axis)


def col(c):
    return slice(c * L, (c + 1) * L)


def kernel(nx, ny, v_in, b_in, k_in, s_in, m_in, f_in, p_in, out,
           v_raw, b_raw, k_raw, s_raw, m_raw, f_raw, p_raw,
           v0, v1, v2, v3, rhs, const, res, lifted, part0, part1, part2, part3, prod, prod1,
           hx0, hy0, hx1, hy1, hpx1, hpy1, hx2, hy2, hpx3, hpy3, hx3, hy3, edge1, edge3, corner2, corner_c2, hk, hkc, c1, c2, hc1, hc2,
           gst, rst, pst, qst, gpx, gpy, ghx, ghy, alpha, calpha, krow, local_sem, send_sem, recv_sem):
    gx, gy = lax.axis_index("gx"), lax.axis_index("gy")
    has = {(-1, 0): gx > 0, (1, 0): gx < nx - 1, (0, -1): gy > 0, (0, 1): gy < ny - 1}
    for dx in (-1, 1):
        for dy in (-1, 1):
            has[dx, dy] = jnp.logical_and(has[dx, 0], has[0, dy])
    faces = ((0, -1), (0, 1), (-1, 0), (1, 0))
    diagonals = ((-1, -1), (-1, 1), (1, -1), (1, 1))
    odd = lax.rem(gx, 2)
    away_x = gx + 2 * odd - 1
    has_away = jnp.logical_and(away_x >= 0, away_x < nx)

    loads = [pltpu.make_async_copy(src, dst, local_sem.at[i]) for i, (src, dst) in enumerate(
        ((k_in, k_raw), (v_in, v_raw), (m_in, m_raw), (s_in, s_raw), (f_in, f_raw), (b_in, b_raw), (p_in, p_raw)))]
    barrier = pltpu.get_barrier_semaphore()
    for d in faces:
        @pl.when(has[d])
        def _(d=d):
            pl.semaphore_signal(barrier, inc=1, device_id=(gx + d[0], gy + d[1]), device_id_type=MESH)
    for load in loads[:2]:
        load.start()

    sent = []

    def put(src, dst, device, out_if, in_if):
        slot = len(sent)
        copy = pltpu.make_async_remote_copy(
            src_ref=src, dst_ref=dst, send_sem=send_sem.at[slot], recv_sem=recv_sem.at[slot],
            device_id=device, device_id_type=MESH)
        pl.when(out_if)(copy.start)
        sent.append((copy, out_if))
        return copy, in_if

    def send(src, dst, d):
        return put(src, dst, (gx + d[0], gy + d[1]), has[d], has[-d[0], -d[1]])

    def relay(src, dst, j):
        there = has[0, 2 * j - 1]
        return put(src, dst, (gx + 1 - 2 * odd, gy), there, there)

    def arrive(*copies):
        for copy, in_if in copies:
            pl.when(in_if)(copy.wait_recv)

    def send_y(v, hy):
        return [send(v.at[:, :, col(3)], hy.at[0], (0, 1)), send(v.at[:, :, col(0)], hy.at[1], (0, -1))]

    def send_x(v, hx):
        return [send(v.at[1], hx.at[0], (1, 0)), send(v.at[0], hx.at[1], (-1, 0))]

    def send_edges(v, edge):
        return [put(v.at[odd, :, col(3 if dy > 0 else 0)], edge.at[2 * (1 - odd) + (1 - dy) // 2], (away_x, gy + dy),
                    jnp.logical_and(has_away, has[0, dy]), jnp.logical_and(has_away, has[0, -dy])) for dy in (-1, 1)]

    def send_tile(c, h):
        return (send(c, h.at[0], (0, 1)), send(c, h.at[1], (0, -1)), send(c, h.at[2], (1, 0)), send(c, h.at[3], (-1, 0)))

    loads[1].wait()
    for load in loads[2:]:
        load.start()
    for c in range(8):
        v0[c // 4, :, col(c % 4)] = v_raw[pl.ds(c, D, stride=8), :]
    loads[0].wait()
    count = has[-1, 0].astype(jnp.int32) + has[1, 0].astype(jnp.int32) + has[0, -1].astype(jnp.int32) + has[0, 1].astype(jnp.int32)
    pl.semaphore_wait(barrier, count)
    kcopies = send_tile(k_raw, hk)
    first = send_y(v0, hy0) + send_x(v0, hx0)

    for d, y_at, x_at in (((0, -1), 0, None), ((0, 1), 1, None), ((-1, 0), None, 0), ((1, 0), None, 1)):
        @pl.when(jnp.logical_not(has[d]))
        def _(y_at=y_at, x_at=x_at):
            if x_at is None:
                for ref in (hy0, hy1, hpy1, hpy3):
                    ref[y_at] = jnp.zeros_like(ref[y_at])
                for ref in (hk, hc1, hc2):
                    ref[y_at] = jnp.zeros_like(ref[y_at])
                for i in range(2):
                    for ref in (edge1, edge3, corner2, corner_c2, hkc):
                        ref[2 * i + y_at] = jnp.zeros_like(ref[0])
            else:
                for ref in (hx0, hx1, hpx1, hpx3):
                    ref[x_at] = jnp.zeros_like(ref[x_at])
                for ref in (hk, hc1, hc2):
                    ref[2 + x_at] = jnp.zeros_like(ref[0])
                for j in range(2):
                    for ref in (edge1, edge3, corner2, corner_c2, hkc):
                        ref[2 * x_at + j] = jnp.zeros_like(ref[0])

    lane = lax.broadcasted_iota(jnp.int32, (D, L), 1)
    low_half = lane < D
    even = lax.rem(lane, 2) == 0
    row_even = even[:1]

    def twice(w):
        return jnp.concatenate([w, w], axis=1)

    def put_left(ref, rows, w, lanes=0):
        hi, lo = parts(w)
        both = jnp.where(low_half, hi.astype(F32), lo.astype(F32)).astype(BF16)
        ref[rows, lanes:lanes + L] = both
        ref[rows, lanes + L:lanes + 2 * L] = both

    def block(i):
        return slice(i * D, (i + 1) * D)

    for i in (2, 3, 4):
        loads[i].wait()
    m_hi, m_lo = parts(twice(m_raw[...]))
    m_both = jnp.where(low_half, m_hi.astype(F32), m_lo.astype(F32)).astype(BF16)
    m_left = jnp.concatenate([m_both, m_both], axis=1)
    order = ((XLO, 0), (XHI, 1), (YLO, 2), (YHI, 3), (ZLO, 4), (ZHI, 5))
    raw = {CEN: twice(s_raw[...])}
    for blk, face in order:
        raw[blk] = twice(f_raw[face])
    stacked = jnp.concatenate([raw[blk] for blk in range(7)], axis=1)
    folded = dot(m_left, split_rows(stacked))
    eye = (lax.rem(lane, D) == lax.broadcasted_iota(jnp.int32, (D, L), 0)).astype(F32)
    for blk in range(7):
        w = folded[:, col(blk)]
        put_left(gst, block(blk), eye - w if blk == CEN else w)

    loads[5].wait()
    k8 = k_raw[...]
    inv8 = 1.0 / k8
    for c in range(8):
        krow[c // 4, 0:1, col(c % 4)] = k8[c:c + 1]
        krow[c // 4, 1:2, col(c % 4)] = inv8[c:c + 1]
        rhs[c // 4, :, col(c % 4)] = b_raw[pl.ds(c, D, stride=8), :]
    for x in range(2):
        const[x] = dot(m_left, split_rows(rhs[x])) * krow[x, 1:2, :]

    def weigh(ke, kn):
        return jnp.where(kn > 0, 2.0 * kn / (ke + kn), 0.0)

    def weight(blk, c):
        return alpha[blk, c:c + 1, :]

    for blk in range(7):
        put_left(rst, block(blk), -raw[blk] if blk == CEN else raw[blk])
    loads[6].wait()
    twins, doubled = [], []
    for abc in range(8):
        w = twice(p_raw[abc])
        doubled.append(w)
        put_left(pst, block(abc), w)
        hi, lo = parts(w)
        right_form = jnp.concatenate([hi, lo], axis=1)
        twins += [right_form, right_form]
    for ref, i, blk, chosen in ((gpx, 0, XLO, (4, 5, 6, 7)), (gpx, 1, XHI, (0, 1, 2, 3)),
                                (gpy, 0, YLO, (2, 3, 6, 7)), (gpy, 1, YHI, (0, 1, 4, 5))):
        both = dot(gst[block(blk), :], split_rows(jnp.concatenate([doubled[abc] for abc in chosen], axis=1)))
        for n in range(4):
            put_left(ref.at[i], block(n), both[:, col(n)])
    folded_p = lax.dot_general(m_left, jnp.concatenate(twins, axis=0), (((1,), (1,)), ((), ())),
                               preferred_element_type=F32)
    for abc in range(8):
        ab, c = divmod(abc, 2)
        put_left(qst, block(c), folded_p[:, col(abc)], 2 * L * ab)

    row8 = lax.broadcasted_iota(jnp.int32, (8, L), 0)
    lane8 = lax.broadcasted_iota(jnp.int32, (8, L), 1)
    y8 = lax.rem(row8, 4)
    own_neighbours = {
        XLO: roll(k8, 4, 0),
        XHI: roll(k8, 4, 0),
        YLO: roll(k8, 1, 0),
        YHI: roll(k8, -1, 0),
        ZLO: jnp.where(lane8 == 0, 0.0, roll(k8, 1)),
        ZHI: jnp.where(lane8 == L - 1, 0.0, roll(k8, -1)),
    }
    for blk, kn in own_neighbours.items():
        alpha[blk] = weigh(k8, kn)

    ends_first = (0, 4, 3, 7, 1, 5, 2, 6)

    def own_part(target, v, stack, base, scale, prod, wide, ends_done=None):
        for x in range(2):
            rows = slice(0, 7 * D) if wide else slice(x * D, (6 + x) * D)
            prod[x, rows, :] = dot(stack[rows, :], split_rows(v[x]))
        for c in ends_first:
            x, y = divmod(c, 4)

            def term(blk, x, y):
                return prod[x, block(blk), col(y)]

            acc = term(CEN, x, y)
            acc += weight(ZLO, c) * roll(term(ZLO, x, y), 1)
            acc += weight(ZHI, c) * roll(term(ZHI, x, y), -1)
            if x == 0:
                acc += weight(XHI, c) * term(XHI, 1, y)
            else:
                acc += weight(XLO, c) * term(XLO, 0, y)
            if y > 0:
                acc += weight(YLO, c) * term(YLO, x, y - 1)
            if y < 3:
                acc += weight(YHI, c) * term(YHI, x, y + 1)
            if scale is not None:
                acc = acc * scale[x, 0:1, col(y)]
            target[x, :, col(y)] = base[x, :, col(y)] + acc
            if c == 7 and ends_done is not None:
                ends_done()

    def halo_products(stack, hx, hy, copies=(), passed_on=None):
        found_x, found_y = [], []
        arrive(*copies[:2])
        for j in range(2):
            if passed_on is not None:
                passed_on(j)
        arrive(*copies[2:])
        for j in range(2):
            found_y.append(dot(stack[block((YLO, YHI)[j]), :],
                               split_rows(jnp.concatenate([hy[j, 0], hy[j, 1]], axis=1))))
        for i in range(2):
            found_x.append(dot(stack[block((XLO, XHI)[i]), :], split_rows(hx[i])))
        return found_x + found_y

    def halo_part(target, part, products, scale, ends_done=None):
        from_xlo, from_xhi, from_ylo, from_yhi = products
        for c in ends_first:
            x, y = divmod(c, 4)
            acc = weight(XLO, c) * from_xlo[:, col(y)] if x == 0 else weight(XHI, c) * from_xhi[:, col(y)]
            if y == 0:
                acc += weight(YLO, c) * from_ylo[:, col(x)]
            if y == 3:
                acc += weight(YHI, c) * from_yhi[:, col(x)]
            if scale is not None:
                acc = acc * scale[x, 0:1, col(y)]
            value = part[x, :, col(y)] + acc
            if target is out:
                out[pl.ds(c, D, stride=8), :] = value
            else:
                target[x, :, col(y)] = value
            if c == 7 and ends_done is not None:
                ends_done()

    def complete_halo(hx, hy, hpx, hpy, edge, copies):
        arrive(*copies)

        def edges(i, j):
            return split_rows(jnp.concatenate([edge[i], edge[j]], axis=1))

        from_edge = {XLO: dot(gst[block(XLO), :], edges(0, 1)), XHI: dot(gst[block(XHI), :], edges(2, 3)),
                     YLO: dot(gst[block(YLO), :], edges(0, 2)), YHI: dot(gst[block(YHI), :], edges(1, 3))}
        kx, ky = (kxlo, kxhi), (kylo, kyhi)
        for i in range(2):
            mine, theirs = ((XLO, XHI), (XHI, XLO))[i]
            for y in range(4):
                c = 4 * i + y
                value = hpx[i, :, col(y)] + (2.0 - weight(mine, c)) * prod1[i, block(theirs), col(y)]
                if y in (0, 3):
                    j = y // 3
                    w = weigh(kx[i][4 * (1 - i) + y:4 * (1 - i) + y + 1],
                              hkc[2 * i + j][4 * (1 - i) + 3 - y:4 * (1 - i) + 4 - y])
                    value += w * from_edge[(YLO, YHI)[j]][:, col(i)]
                hx[i, :, col(y)] = value
        for j in range(2):
            mine, theirs = ((YLO, YHI), (YHI, YLO))[j]
            y = 3 * j
            for x in range(2):
                value = hpy[j, x] + (2.0 - weight(mine, 4 * x + y)) * prod1[x, block(theirs), col(y)]
                e, n = 4 * x + 3 - y, 4 * (1 - x) + 3 - y
                w = weigh(ky[j][e:e + 1], hkc[2 * x + j][n:n + 1])
                value += w * from_edge[(XLO, XHI)[x]][:, col(j)]
                hy[j, x] = value

    later = []
    own_part(part0, v0, gst, const, None, prod, False)
    arrive(*kcopies)
    kylo, kyhi, kxlo, kxhi = (hk[i] for i in range(4))
    neighbours = {
        XLO: jnp.where(row8 < 4, roll(kxlo, 4, 0), own_neighbours[XLO]),
        XHI: jnp.where(row8 < 4, own_neighbours[XHI], roll(kxhi, 4, 0)),
        YLO: jnp.where(y8 == 0, roll(kylo, -3, 0), own_neighbours[YLO]),
        YHI: jnp.where(y8 == 3, roll(kyhi, 3, 0), own_neighbours[YHI]),
    }
    for blk, kn in neighbours.items():
        alpha[blk] = weigh(k8, kn)


    def ends_of_v1():
        later.extend(send_edges(v1, edge1) + send_y(v1, hy1))

    halo_part(v1, part0, halo_products(gst, hx0, hy0, first), None, ends_of_v1)
    edges1, second = later[:2], later[2:]
    second = second + send_x(v1, hx1)
    parts1 = [send(k_raw, hkc.at[(1 - dx) + (1 - dy) // 2], (dx, dy)) for dx, dy in diagonals]
    own_part(part1, v1, gst, const, None, prod1, True, lambda: parts1.extend(send_y(part1, hpy1)))
    parts1 += send_x(part1, hpx1)

    def coarse_k(k):
        def one(q):
            s = (k[2 * q:2 * q + 1] + k[2 * q + 1:2 * q + 2]) + (k[4 + 2 * q:5 + 2 * q] + k[5 + 2 * q:6 + 2 * q])
            return (s + roll(s, -1)) * 0.125

        return jnp.where(row_even, one(0), roll(one(1), 1))

    kc = coarse_k(k8)
    lane1 = lax.broadcasted_iota(jnp.int32, (1, L), 1)
    cylo, cyhi = coarse_k(kylo), coarse_k(kyhi)
    coarse_neighbours = {
        XLO: coarse_k(kxlo),
        XHI: coarse_k(kxhi),
        YLO: jnp.where(row_even, roll(cylo, -1), roll(kc, 1)),
        YHI: jnp.where(row_even, roll(kc, -1), roll(cyhi, 1)),
        ZLO: jnp.where(lane1 < 2, 0.0, roll(kc, 2)),
        ZHI: jnp.where(lane1 >= L - 2, 0.0, roll(kc, -2)),
    }
    for blk, kn in coarse_neighbours.items():
        calpha[blk:blk + 1, :] = weigh(kc, kn)
    inv_kc = 1.0 / kc

    halo_part(v2, part1, halo_products(gst, hx1, hy1, second, lambda j: parts1.append(
        relay(hy1.at[j, 1 - odd], edge1.at[2 * odd + j], j))), None)

    own_part(part2, v2, rst, rhs, krow, prod, False)
    complete_halo(hx2, hy2, hpx1, hpy1, edge1, edges1 + parts1)
    halo_part(res, part2, halo_products(rst, hx2, hy2), krow)
    r_right = [split_rows(res[x]) for x in range(2)]
    columns = []
    for a in range(2):
        for b in range(2):
            columns.append(jnp.concatenate([r_right[a][:, col(b)], r_right[a][:, col(2 + b)]], axis=1))
    t = sum(dot(qst[:, 4 * D * ab:4 * D * (ab + 1)], columns[ab]) for ab in range(4))
    packed = jnp.where(even, t[:D, :L] + roll(t[D:, :L], -1), roll(t[:D, L:], 1) + t[D:, L:])
    c1[...] = packed * inv_kc

    third = send_tile(c1, hc1)
    corners2 = [relay(hy2.at[j, 1 - odd], corner2.at[2 * odd + j], j) for j in range(2)]
    for i, product in enumerate(halo_products(gst, hx2, hy2)):
        if i < 2:
            ghx[i] = product
        else:
            ghy[i - 2] = product
    corr1 = c1[...]
    y = dot(gst[D:4 * D, :], split_rows(corr1))
    acc = corr1 + y[:D]
    acc += calpha[ZLO:ZLO + 1, :] * roll(y[D:2 * D], 2)
    acc += calpha[ZHI:ZHI + 1, :] * roll(y[2 * D:], -2)
    arrive(*third)
    acc += calpha[XLO:XLO + 1, :] * dot(gst[block(XLO), :], split_rows(hc1[2]))
    acc += calpha[XHI:XHI + 1, :] * dot(gst[block(XHI), :], split_rows(hc1[3]))
    below = jnp.where(even, roll(hc1[0], -1), roll(corr1, 1))
    acc += calpha[YLO:YLO + 1, :] * dot(gst[block(YLO), :], split_rows(below))
    above = jnp.where(even, roll(corr1, -1), roll(hc1[1], 1))
    acc += calpha[YHI:YHI + 1, :] * dot(gst[block(YHI), :], split_rows(above))
    c2[...] = acc

    fourth = send_tile(c2, hc2)

    def lift(o, q):
        if q == 0:
            return jnp.where(even, o[:D], roll(o[D:], 1))
        return jnp.where(even, roll(o[:D], -1), o[D:])

    def pair(o, i):
        return o[2 * i * D:2 * (i + 1) * D]

    o = dot(pst[...], split_rows(c2[...]))
    for c in range(8):
        x, y = divmod(c, 4)
        q, b = divmod(y, 2)
        lifted[x, :, col(y)] = v2[x, :, col(y)] + lift(pair(o, 2 * x + b), q)
    parts3 = send_edges(lifted, edge3)
    own_part(part3, lifted, gst, const, None, prod1, True, lambda: parts3.extend(send_y(part3, hpy3)))
    parts3 += send_x(part3, hpx3)
    products = []
    passed = []
    arrive(*fourth[:2])
    for j in range(2):
        passed.append(relay(hc2.at[j], corner_c2.at[2 * odd + j], j))
    arrive(*fourth[2:])
    for j in range(2):
        o = dot(gpy[j], split_rows(hc2[j]))
        products.append(ghy[j] + jnp.concatenate([lift(pair(o, x), 1 - j) for x in range(2)], axis=1))
    for i in range(2):
        o = dot(gpx[i], split_rows(hc2[2 + i]))
        products.insert(i, ghx[i] + jnp.concatenate([lift(pair(o, y % 2), y // 2) for y in range(4)], axis=1))
    halo_part(v3, part3, products, None)
    own_part(part0, v3, gst, const, None, prod, False)
    arrive(*corners2, *passed)
    for j in range(2):
        at = 2 * (1 - odd) + j
        rows = pl.ds(pl.multiple_of(odd * 4 * D + (1 - j) * L, L), L)
        edge3[at] = corner2[at] + lift(dot(pst[rows, :], split_rows(corner_c2[at])), 1 - j)
    complete_halo(hx3, hy3, hpx3, hpy3, edge3, parts3)
    halo_part(out, part0, halo_products(gst, hx3, hy3), None)
    for copy, out_if in sent:
        pl.when(out_if)(copy.wait_send)


def on_device(nx, ny, start_field, right_side, coefficient, stiffness, smoother, face_coupling, prolongation):
    flat = lambda x: x.reshape(8 * D, L)
    field = pltpu.VMEM((2, D, 4 * L), F32)
    small = pltpu.VMEM((D, L), F32)
    four = pltpu.VMEM((4, D, L), F32)
    kfour = pltpu.VMEM((4, 8, L), F32)
    xhalo = pltpu.VMEM((2, D, 4 * L), F32)
    yhalo = pltpu.VMEM((2, 2, D, L), F32)
    sends = 42

    def body(*refs):
        kernel(nx, ny, *refs)

    result = pl.pallas_call(
        body,
        out_shape=jax.ShapeDtypeStruct((8 * D, L), F32),
        in_specs=[pl.BlockSpec(memory_space=pltpu.HBM)] * 7,
        out_specs=pl.BlockSpec(memory_space=pltpu.VMEM),
        scratch_shapes=[
            pltpu.VMEM((8 * D, L), F32), pltpu.VMEM((8 * D, L), F32), pltpu.VMEM((8, L), F32),
            pltpu.VMEM((D, D), F32), pltpu.VMEM((D, D), F32), pltpu.VMEM((6, D, D), F32), pltpu.VMEM((8, D, D), F32),
            *[field] * 12, pltpu.VMEM((2, 7 * D, 4 * L), F32), pltpu.VMEM((2, 7 * D, 4 * L), F32),
            *[xhalo, yhalo] * 6, four, four, four, four, kfour, kfour, small, small, four, four,
            pltpu.VMEM((7 * D, 4 * D), BF16), pltpu.VMEM((7 * D, 4 * D), BF16),
            pltpu.VMEM((8 * D, 4 * D), BF16), pltpu.VMEM((2 * D, 16 * D), BF16),
            pltpu.VMEM((2, 4 * D, 4 * D), BF16), pltpu.VMEM((2, 4 * D, 4 * D), BF16), xhalo, pltpu.VMEM((2, D, 2 * L), F32),
            pltpu.VMEM((7, 8, L), F32), pltpu.VMEM((8, L), F32), pltpu.VMEM((2, 8, 4 * L), F32),
            pltpu.SemaphoreType.DMA((7,)), pltpu.SemaphoreType.DMA((sends,)), pltpu.SemaphoreType.DMA((sends,)),
        ],
        compiler_params=pltpu.CompilerParams(
            collective_id=0, has_side_effects=True, vmem_limit_bytes=40 * 2**20),
    )(*(pltpu.with_memory_space_constraint(x, pltpu.HBM) for x in (
        flat(start_field), flat(right_side), coefficient.reshape(8, L), stiffness, smoother, face_coupling,
        prolongation.reshape(8, D, D))))
    return result.reshape(start_field.shape)


def solution(mesh):
    nx, ny = mesh.shape["gx"], mesh.shape["gy"]
    placed = (P(None, "gx", "gy", None), P(None, "gx", "gy", None), P("gx", "gy", None), P(), P(), P(), P())

    def run(*args):
        return on_device(nx, ny, *args)

    return jax.shard_map(
        run, mesh=mesh, in_specs=placed, out_specs=P(None, "gx", "gy", None), check_vma=False)
```
